128 devices in a mesh: dp: 16 (over x, y_lo, core), sample: 8 (over y_hi, z).
Axes of the slice: x: 4, y: 4 (y_hi: 2, y_lo: 2; y = y_hi * 2 + y_lo), z: 4, core: 2. Of those that a mesh axis runs over, the one named last changes fastest.
Arguments:
- query_vectors: bfloat16 [16, 16, 256, 1024], P('dp', 'sample'), may hold values from -6 to 6
- key_vectors: bfloat16 [16, 16, 256, 1024], P('dp', 'sample'), may hold values from -6 to 6
- value_vectors: bfloat16 [16, 16, 256, 2048], P('dp', 'sample'), may hold values from -6 to 6
- output_gates: bfloat16 [16, 16, 256, 2048], P('dp', 'sample'), may hold values from -6 to 6
- beta_logits: bfloat16 [16, 16, 16, 256], P('dp', 'sample'), may hold values from -6 to 6
- decay_logits: bfloat16 [16, 16, 16, 256], P('dp', 'sample'), may hold values from -6 to 6
- decay_rates: float32 [16], replicated, may hold values from 0.003 to 0.08
- norm_gain: float32 [128], replicated, may hold values from 0.5 to 1.5
- prefix_states: float32 [16, 16, 128, 128], P('dp', 'sample'), may hold values from -4 to 4
- cotangent: bfloat16 [16, 16, 256, 2048], P('dp', 'sample'), may hold values from -6 to 6
- rewards: float32 [16, 16], P('dp', 'sample'), may hold values from -4 to 4
- out_weight: float32 [2048, 2048], P('dp'), may hold values from -0.125 to 0.125
- first_moment: float32 [2048, 2048], P('dp'), may hold values from -4 to 4
- second_moment: float32 [2048, 2048], P('dp'), may hold values from 0.05 to 2
Outputs:
- prefix_grad: float32 [16, 16, 128, 128], P('dp', 'sample')
- weight_new: float32 [2048, 2048], P('dp')
- first_new: float32 [2048, 2048], P('dp')
- second_new: float32 [2048, 2048], P('dp')
The draws below stay inside these ranges and needn't reach their ends.
All inputs are finite; a program needn't handle non-finite values.
Results may differ from the reference program's by a relative error of at most 0.0041.
Values may be sent and summed in bfloat16 or wider, within the bound.
A program may use at most 192 MiB of HBM per device.

```python
import math
import jax
import jax.numpy as jnp
from jax import lax

D = 2048
HEADS = 16
DK = 128
DV = 128
SPAN = 64
LEN = 256
KHEADS = 8
SAMPLES = 16
PROMPTS = 16


def steps_of(rng, dims, cuts, low, top_value):
    gain = 1.0
    for dim, shards_of in cuts:
        steps = jax.random.uniform(jax.random.fold_in(jax.random.fold_in(rng, 6), dim), (shards_of,), jnp.float32, low / len(cuts), top_value / len(cuts))
        gain = gain * jnp.repeat(jnp.exp(steps), dims[dim] // shards_of).reshape((-1,) + (1,) * (len(dims) - 1 - dim))
    return gain


def scatter_about(rng, extent, deviation, bound, split=(), kind=jnp.bfloat16):
    gain = steps_of(rng, extent, split, -0.22, 0.18) if split else 1.0
    entries = jax.random.normal(rng, extent, jnp.float32) * deviation * gain
    return jnp.minimum(jnp.maximum(entries, -bound), bound).astype(kind)


def setup_inputs(seed: int = 0) -> dict:
    key_list = jax.random.split(jax.random.key(seed), 15)
    return {
        "query_vectors": scatter_about(key_list[0], (PROMPTS, SAMPLES, LEN, KHEADS * DK), 1.0, 6.0, ((0, 16), (1, 8))),
        "key_vectors": scatter_about(key_list[1], (PROMPTS, SAMPLES, LEN, KHEADS * DK), 1.0, 6.0, ((0, 16), (1, 8))),
        "value_vectors": scatter_about(key_list[2], (PROMPTS, SAMPLES, LEN, HEADS * DV), 1.0, 6.0, ((0, 16), (1, 8))),
        "output_gates": scatter_about(key_list[3], (PROMPTS, SAMPLES, LEN, HEADS * DV), 1.0, 6.0, ((0, 16), (1, 8))),
        "beta_logits": scatter_about(key_list[4], (PROMPTS, SAMPLES, HEADS, LEN), 1.5, 6.0, ((0, 16), (1, 8))),
        "decay_logits": scatter_about(key_list[5], (PROMPTS, SAMPLES, HEADS, LEN), 1.5, 6.0, ((0, 16), (1, 8))),
        "decay_rates": jnp.clip(jnp.exp(jax.random.uniform(key_list[6], (HEADS,), jnp.float32, math.log(0.003), math.log(0.08))), 0.003, 0.08),
        "norm_gain": jnp.clip(1.0 + 0.1 * jax.random.normal(key_list[7], (DV,), jnp.float32), 0.5, 1.5),
        "prefix_states": scatter_about(key_list[8], (PROMPTS, HEADS, DK, DV), 0.3, 4.0, ((0, 16), (1, 8)), jnp.float32),
        "cotangent": scatter_about(key_list[9], (PROMPTS, SAMPLES, LEN, D), 1.0, 6.0, ((0, 16), (1, 8))),
        "rewards": scatter_about(key_list[10], (PROMPTS, SAMPLES), 1.0, 4.0, ((0, 16), (1, 8)), jnp.float32),
        "out_weight": scatter_about(key_list[11], (HEADS * DV, D), (HEADS * DV) ** -0.5, 0.125, ((0, 16),), jnp.float32),
        "first_moment": scatter_about(key_list[12], (HEADS * DV, D), 0.3, 4.0, ((0, 16),), jnp.float32),
        "second_moment": jnp.clip(jnp.exp(math.log(2.0) - 3.6888794 * jax.random.uniform(key_list[13], (HEADS * DV, D), jnp.float32) ** steps_of(key_list[13], (HEADS * DV, D), ((0, 16),), -0.2, 0.2)), 0.05, 2.0),
    }


TOP_PRECISION = lax.Precision.HIGHEST

def unit_lower_solve(system, targets):
    block_width = system.shape[-1]
    result = targets - jnp.einsum('hij,hjc->hic', system, targets, precision=TOP_PRECISION)
    raised = system
    covered = 2
    while covered < block_width:
        raised = jnp.einsum('hij,hjk->hik', raised, raised, precision=TOP_PRECISION)
        result = result + jnp.einsum('hij,hjc->hic', raised, result, precision=TOP_PRECISION)
        covered = covered * 2
    return result

def span_step(carried_state, pieces):
    query_pieces, keys_c, values_c, beta_gates, decays_c = pieces
    block_width = query_pieces.shape[1]
    cumulative = jnp.cumsum(decays_c, axis=-1)
    row_index = lax.broadcasted_iota(jnp.int32, (block_width, block_width), 0)
    col_index = lax.broadcasted_iota(jnp.int32, (block_width, block_width), 1)
    causal = row_index >= col_index
    strictly = row_index > col_index
    spread = cumulative[:, :, None] - cumulative[:, None, :]
    falloff = jnp.where(causal, jnp.exp(jnp.where(causal, spread, 0.0)), 0.0)
    key_inner = jnp.einsum('hik,hjk->hij', keys_c, keys_c, precision=TOP_PRECISION)
    system = jnp.where(strictly, beta_gates[:, :, None] * key_inner * falloff, 0.0)
    decay_growth = jnp.exp(cumulative)
    targets = jnp.concatenate([(beta_gates * decay_growth)[:, :, None] * keys_c, beta_gates[:, :, None] * values_c], axis=-1)
    triangular_result = unit_lower_solve(system, targets)
    key_dimension = keys_c.shape[-1]
    corrected_values = triangular_result[..., key_dimension:] - jnp.einsum('ale,aew->alw', triangular_result[..., :key_dimension], carried_state, precision=TOP_PRECISION)
    scores = jnp.einsum('hik,hjk->hij', query_pieces, keys_c, precision=TOP_PRECISION) * falloff
    layer_output = jnp.einsum('ale,aew->alw', query_pieces * decay_growth[:, :, None], carried_state, precision=TOP_PRECISION)
    layer_output = layer_output + jnp.einsum('hij,hjv->hiv', scores, corrected_values, precision=TOP_PRECISION)
    final_state = cumulative[:, -1:]
    decayed_keys = keys_c * jnp.exp(final_state - cumulative)[:, :, None]
    carried_state = jnp.exp(final_state)[:, :, None] * carried_state + jnp.einsum('xnd,xnu->xdu', decayed_keys, corrected_values, precision=TOP_PRECISION)
    return (carried_state, layer_output)

def unit_vectors(source, head_count):
    shaped = source.astype(jnp.float32).reshape(source.shape[0], head_count, -1)
    return shaped * lax.rsqrt(lax.optimization_barrier(jnp.sum(shaped * shaped, axis=-1, keepdims=True)) + 1e-06)

def to_blocks(source, block_width):
    length, head_count, inner_width = source.shape
    return source.reshape(length // block_width, block_width, head_count, inner_width).transpose(0, 2, 1, 3)

def gate_blocks(source, block_width):
    head_count, length = source.shape
    return source.reshape(head_count, length // block_width, block_width).transpose(1, 0, 2)

def sequence_core(query_vectors, key_vectors, value_vectors, beta_logits, decay_logits, decay_rates, start_state):
    head_count = beta_logits.shape[0]
    key_heads = head_count // 2
    length = query_vectors.shape[0]
    queries = unit_vectors(query_vectors, key_heads)
    queries = queries * queries.shape[-1] ** (-0.5)
    queries = jnp.repeat(queries, 2, axis=1)
    keys_unit = jnp.repeat(unit_vectors(key_vectors, key_heads), 2, axis=1)
    values_wide = value_vectors.astype(jnp.float32).reshape(length, head_count, -1)
    beta_gates = jax.nn.sigmoid(beta_logits.astype(jnp.float32))
    decays = -decay_rates[:, None] * jax.nn.softplus(decay_logits.astype(jnp.float32))
    pieces = (to_blocks(queries, SPAN), to_blocks(keys_unit, SPAN), to_blocks(values_wide, SPAN), gate_blocks(beta_gates, SPAN), gate_blocks(decays, SPAN))
    closing_state, outputs = lax.scan(span_step, start_state, pieces)
    return outputs.transpose(0, 2, 1, 3).reshape(length, -1)

def gated_norm(core_in, output_gates, norm_gain):
    shaped = core_in.reshape(core_in.shape[:-1] + (-1, norm_gain.shape[0]))
    normed = shaped * lax.rsqrt(lax.optimization_barrier(jnp.mean(shaped * shaped, axis=-1, keepdims=True)) + 1e-06) * norm_gain
    return normed.reshape(core_in.shape) * jax.nn.silu(output_gates.astype(jnp.float32))

def adam_update(weight, first_moment, second_moment, gradient):
    first_new = 0.9 * first_moment + 0.1 * gradient
    second_new = 0.95 * second_moment + 0.05 * gradient * gradient
    direction = first_new / (1.0 - 0.9 ** 10) / (jnp.sqrt(second_new / (1.0 - 0.95 ** 10)) + 1e-08)
    weight_new = weight - 0.001 * (direction + 0.1 * weight)
    return (weight_new, first_new, second_new)

def widened(source):
    return lax.optimization_barrier(source).astype(jnp.float32)

def reference(query_vectors, key_vectors, value_vectors, output_gates, beta_logits, decay_logits, decay_rates, norm_gain, prefix_states, cotangent, rewards, out_weight, first_moment, second_moment):
    centre = lax.optimization_barrier(jnp.mean(rewards, axis=1, keepdims=True))
    spread = jnp.sqrt(lax.optimization_barrier(jnp.mean((rewards - centre) * (rewards - centre), axis=1, keepdims=True)))
    coefficient = (rewards - centre) / jnp.maximum(spread, 0.6) / LEN
    weight_wide = widened(out_weight.astype(jnp.bfloat16))
    run_samples = jax.vmap(sequence_core, in_axes=(0, 0, 0, 0, 0, None, None))

    def one_prompt(running, items):
        queries_p, keys_p, values_p, gates_p, betas_p, decays_p, start_p, cot_p, coef_p = items
        weighted = (cot_p.astype(jnp.float32) * coef_p[:, None, None]).astype(jnp.bfloat16)
        core_out, pull_state = jax.vjp(lambda start_in: run_samples(queries_p, keys_p, values_p, betas_p, decays_p, decay_rates, start_in), start_p)
        mixed_wide, pull_norm = jax.vjp(lambda core_in: gated_norm(core_in, gates_p, norm_gain), core_out)
        mixed_rows = widened(mixed_wide.astype(jnp.bfloat16)).reshape(-1, mixed_wide.shape[-1])
        flat_weighted = widened(weighted).reshape(-1, weighted.shape[-1])
        back_rows = jnp.dot(flat_weighted, weight_wide.T, preferred_element_type=jnp.float32)
        core_grad, = pull_norm(back_rows.reshape(core_out.shape))
        start_grad, = pull_state(core_grad)
        running = running + jnp.dot(mixed_rows.T, flat_weighted, preferred_element_type=jnp.float32)
        return (running, start_grad)
    items = (query_vectors, key_vectors, value_vectors, output_gates, beta_logits, decay_logits, prefix_states, cotangent, coefficient)
    gradient, prefix_grad = lax.scan(one_prompt, jnp.zeros(out_weight.shape, jnp.float32), items)
    weight_new, first_new, second_new = adam_update(out_weight, first_moment, second_moment, gradient)
    return (prefix_grad, weight_new, first_new, second_new)
```

```python
import functools
import jax
import jax.numpy as jnp
from jax import lax
from jax.experimental import pallas as pl
from jax.experimental.pallas import tpu as pltpu
from jax.sharding import PartitionSpec as P

LEN = 256
F32 = jnp.float32
BF = jnp.bfloat16


def dot(a, b, dims=((1,), (0,))):
    return lax.dot_general(a, b, (dims, ((), ())), preferred_element_type=F32)


def iota(shape, dim):
    return lax.broadcasted_iota(jnp.int32, shape, dim)


def split(x):
    high = x.astype(BF)
    return high, (x - high.astype(F32)).astype(BF)


def odd_rows(x, width):
    n = x.shape[0] // (2 * width)
    return x.reshape((n, 2, width) + x.shape[1:])[:, 1].reshape((n * width,) + x.shape[1:])


def put_odd(x, rows, width):
    n = x.shape[0] // (2 * width)
    parted = x.reshape((n, 2, width) + x.shape[1:])
    rows = rows.reshape((n, width) + x.shape[1:])
    return jnp.stack([parted[:, 0], parted[:, 1] - rows], axis=1).reshape(x.shape)


def inverses(systems, masks_ref):
    count = len(systems)
    eye = masks_ref[8]
    results = [eye - a * masks_ref[0] for a in systems]
    for level in range(1, 8):
        width = 1 << level
        mask = masks_ref[level]
        if width < 16:
            lefts = [dot(results[i], systems[i] * mask).astype(BF) for i in range(count)]
            fixes = [dot(lefts[i], results[i]).astype(BF) for i in range(count)]
            results = [results[i] - fixes[i] for i in range(count)]
        else:
            lefts = [dot(odd_rows(results[i], width), systems[i] * mask).astype(BF) for i in range(count)]
            fixes = [dot(lefts[i], results[i]).astype(BF) for i in range(count)]
            results = [put_odd(results[i], fixes[i], width) for i in range(count)]
    return [r - eye for r in results]


def forward_kernel(samples, q_ref, k_ref, v_ref, g_ref, small_ref, gain_ref, state_ref, mixed_ref, core_ref, read_ref, masks_ref):
    rows = iota((LEN, LEN), 0)
    cols = iota((LEN, LEN), 1)

    @pl.when(pl.program_id(0) == 0)
    def _():
        for level in range(8):
            same = (rows >> (level + 1)) == (cols >> (level + 1))
            below = (rows >> level) > (cols >> level)
            masks_ref[level] = jnp.where(same & below, 1.0, 0.0).astype(BF)
        masks_ref[8] = jnp.where(rows == cols, 1.0, 0.0).astype(BF)
        masks_ref[9] = jnp.where(rows <= cols, 1.0, 0.0).astype(BF)

    small = small_ref[0]
    first = small.astype(BF)
    rest = small - first.astype(F32)
    second = rest.astype(BF)
    third = (rest - second.astype(F32)).astype(BF)
    upper = masks_ref[9]
    running = dot(first, upper) + dot(second, upper) + dot(third, upper)
    mixed_small = jnp.where(iota(small.shape, 0) < 2 * samples, jax.nn.sigmoid(small), running)
    columns = mixed_small.T
    causal = rows >= cols
    strict = rows > cols
    diagonal = rows == cols
    gain = gain_ref[...]

    systems, scores, gates, rights, queries = [], [], [], [], []
    for s in range(samples):
        q = q_ref[s]
        k = k_ref[s]
        qk = dot(jnp.concatenate([k, q], axis=0), k, ((1,), (1,)))
        kk, qk = qk[:LEN], qk[LEN:]
        kf = k.astype(F32)
        qf = q.astype(F32)
        k_row = lax.rsqrt(jnp.sum(jnp.where(diagonal, kk, 0.0), axis=0, keepdims=True) + 1e-6)
        k_col = lax.rsqrt(jnp.sum(kf * kf, axis=1, keepdims=True) + 1e-6)
        q_col = lax.rsqrt(jnp.sum(qf * qf, axis=1, keepdims=True) + 1e-6) * (128 ** -0.5)
        kk = kk * k_row
        qk = qk * k_row
        for r in range(2):
            i = 2 * s + r
            beta = columns[:, i:i + 1]
            c_col = columns[:, 2 * samples + i:2 * samples + i + 1]
            c_row = mixed_small[2 * samples + i:2 * samples + i + 1]
            falloff = jnp.exp(jnp.where(causal, c_col - c_row, 0.0))
            a = jnp.where(strict, falloff * kk * (beta * k_col), 0.0)
            p = jnp.where(causal, falloff * qk * q_col, 0.0)
            growth = jnp.exp(c_col)
            v = v_ref[s, :, 128 * r:128 * r + 128].astype(F32)
            systems.append(a.astype(BF))
            scores.append(split(p))
            rights.append(jnp.concatenate([beta * v, (beta * growth * k_col) * kf], axis=1))
            queries.append((growth * q_col) * qf)
    solved = inverses(systems, masks_ref)
    for s in range(samples):
        for r in range(2):
            i = 2 * s + r
            u = rights[i] + dot(solved[i], rights[i].astype(BF))
            u_high, u_low = split(u)
            p_high, p_low = scores[i]
            pu = dot(p_high, u_high) + (dot(p_low, u_high) + dot(p_high, u_low))
            read = queries[i] - pu[:, 128:]
            read16 = read.astype(BF)
            core = pu[:, :128] + dot(read16, state_ref[r].astype(BF))
            gate = g_ref[s, :, 128 * r:128 * r + 128].astype(F32)
            scale = lax.rsqrt(jnp.mean(core * core, axis=1, keepdims=True) + 1e-6)
            mixed_ref[s, :, 128 * r:128 * r + 128] = (core * scale * gain * (gate * jax.nn.sigmoid(gate))).astype(BF)
            core_ref[s, :, 128 * r:128 * r + 128] = core.astype(BF)
            read_ref[s, :, 128 * r:128 * r + 128] = read16


def forward(q, k, v, g, small, gain, state, samples=2):
    kheads = q.shape[2] // 128
    wide = pl.BlockSpec((samples, LEN, 256), lambda i: (0, 0, i))
    narrow = pl.BlockSpec((samples, LEN, 128), lambda i: (0, 0, i))
    out = jax.ShapeDtypeStruct((samples, LEN, kheads * 256), BF)
    return pl.pallas_call(
        functools.partial(forward_kernel, samples),
        grid=(kheads,),
        in_specs=[
            narrow, narrow, wide, wide,
            pl.BlockSpec((1, 4 * samples, LEN), lambda i: (i, 0, 0)),
            pl.BlockSpec((1, 128), lambda i: (0, 0)),
            pl.BlockSpec((2, 128, 128), lambda i: (i, 0, 0)),
        ],
        out_specs=[wide, wide, wide],
        out_shape=[out, out, out],
        scratch_shapes=[pltpu.VMEM((10, LEN, LEN), BF)],
        compiler_params=pltpu.CompilerParams(vmem_limit_bytes=48 * 1024 * 1024),
        cost_estimate=pl.CostEstimate(flops=16_000_000_000, bytes_accessed=14_000_000, transcendentals=0),
    )(q, k, v, g, small, gain, state)


def backward_kernel(samples, back_ref, g_ref, core_ref, read_ref, gain_ref, out_ref):
    gain = gain_ref[...]
    total = jnp.zeros((128, 128), F32)
    for s in range(samples):
        core = core_ref[s].astype(F32)
        gate = g_ref[s].astype(F32)
        scale = lax.rsqrt(jnp.mean(core * core, axis=1, keepdims=True) + 1e-6)
        normed = core * scale
        lifted = back_ref[s] * gain * (gate * jax.nn.sigmoid(gate))
        core_grad = scale * (lifted - normed * jnp.mean(lifted * normed, axis=1, keepdims=True))
        total = total + dot(read_ref[s], core_grad.astype(BF), ((0,), (0,)))
    out_ref[0] = total


def backward(back, g, core, read, gain, samples=2):
    heads = g.shape[2] // 128
    block = pl.BlockSpec((samples, LEN, 128), lambda i: (0, 0, i))
    return pl.pallas_call(
        functools.partial(backward_kernel, samples),
        grid=(heads,),
        in_specs=[block, block, block, block, pl.BlockSpec((1, 128), lambda i: (0, 0))],
        out_specs=pl.BlockSpec((1, 128, 128), lambda i: (i, 0, 0)),
        out_shape=jax.ShapeDtypeStruct((heads, 128, 128), F32),
        compiler_params=pltpu.CompilerParams(vmem_limit_bytes=48 * 1024 * 1024),
        cost_estimate=pl.CostEstimate(flops=500_000_000, bytes_accessed=12_000_000, transcendentals=0),
    )(back, g, core, read, gain)


def adam_update(weight, first_moment, second_moment, gradient):
    first_new = 0.9 * first_moment + 0.1 * gradient
    second_new = 0.95 * second_moment + 0.05 * gradient * gradient
    direction = first_new / (1.0 - 0.9**10) / (jnp.sqrt(second_new / (1.0 - 0.95**10)) + 1e-08)
    weight_new = weight - 0.001 * (direction + 0.1 * weight)
    return (weight_new, first_new, second_new)


def local(
    query_vectors,
    key_vectors,
    value_vectors,
    output_gates,
    beta_logits,
    decay_logits,
    decay_rates,
    norm_gain,
    prefix_states,
    cotangent,
    rewards,
    out_weight,
    first_moment,
    second_moment,
):
    samples = rewards.shape[1]
    heads = beta_logits.shape[2]
    all_rewards = lax.all_gather(rewards, "sample", axis=1, tiled=True)
    centre = jnp.mean(all_rewards, axis=1, keepdims=True)
    spread = jnp.sqrt(jnp.mean((all_rewards - centre) * (all_rewards - centre), axis=1, keepdims=True))
    coefficient = (rewards - centre) / jnp.maximum(spread, 0.6) / LEN
    weighted = (cotangent[0].astype(F32) * coefficient[0, :, None, None]).astype(BF)
    states = lax.all_gather(prefix_states[0], "sample", axis=0, tiled=True)
    weight16 = lax.all_gather(out_weight.astype(BF), "dp", axis=0, tiled=True)
    decays = -decay_rates[:, None] * jax.nn.softplus(decay_logits[0].astype(F32))

    def by_pair(x):
        return x.reshape(samples, heads // 2, 2, LEN).transpose(1, 0, 2, 3).reshape(heads // 2, 2 * samples, LEN)

    small = jnp.concatenate([by_pair(beta_logits[0].astype(F32)), by_pair(decays)], axis=1)
    gain = norm_gain[None]
    gates = output_gates[0]
    mixed, core, read = forward(
        query_vectors[0], key_vectors[0], value_vectors[0], gates, small, gain, states, samples
    )
    flat_weighted = weighted.reshape(-1, weighted.shape[-1])
    partial = lax.dot_general(
        mixed.reshape(-1, mixed.shape[-1]), flat_weighted, (((0,), (0,)), ((), ())), preferred_element_type=F32
    ).astype(BF)
    partial_rows = lax.psum_scatter(partial, "dp", scatter_dimension=0, tiled=True)
    back = lax.dot_general(
        flat_weighted, weight16, (((1,), (1,)), ((), ())), preferred_element_type=F32
    ).reshape(samples, LEN, -1)
    start_grad = backward(back, gates, core, read, gain, samples)
    prefix_grad = lax.psum_scatter(start_grad, "sample", scatter_dimension=0, tiled=True)[None]
    gradient = lax.psum(partial_rows.astype(F32), "sample")
    return (prefix_grad,) + adam_update(out_weight, first_moment, second_moment, gradient)


def solution(mesh):
    placed = (
        P("dp", "sample", None, None),
        P("dp", "sample", None, None),
        P("dp", "sample", None, None),
        P("dp", "sample", None, None),
        P("dp", "sample", None, None),
        P("dp", "sample", None, None),
        P(),
        P(),
        P("dp", "sample", None, None),
        P("dp", "sample", None, None),
        P("dp", "sample"),
        P("dp", None),
        P("dp", None),
        P("dp", None),
    )
    return jax.shard_map(
        local,
        mesh=mesh,
        in_specs=placed,
        out_specs=(P("dp", "sample", None, None), P("dp", None), P("dp", None), P("dp", None)),
        check_vma=False,
    )
```

```python
import functools
import jax
import jax.numpy as jnp
from jax import lax
from jax.experimental import pallas as pl
from jax.experimental.pallas import tpu as pltpu
from jax.sharding import PartitionSpec as P

LEN = 256
F32 = jnp.float32
BF = jnp.bfloat16
MESH = pl.DeviceIdType.MESH
CHIPS = 8
GROUP = 8


def dot(a, b, dims=((1,), (0,))):
    return lax.dot_general(a, b, (dims, ((), ())), preferred_element_type=F32)


def iota(shape, dim):
    return lax.broadcasted_iota(jnp.int32, shape, dim)


def split(x):
    high = x.astype(BF)
    return high, (x - high.astype(F32)).astype(BF)


def odd_rows(x, width):
    n = x.shape[0] // (2 * width)
    return x.reshape((n, 2, width) + x.shape[1:])[:, 1].reshape((n * width,) + x.shape[1:])


def put_odd(x, rows, width):
    n = x.shape[0] // (2 * width)
    parted = x.reshape((n, 2, width) + x.shape[1:])
    rows = rows.reshape((n, width) + x.shape[1:])
    return jnp.stack([parted[:, 0], parted[:, 1] - rows], axis=1).reshape(x.shape)


def inverses(systems, masks_ref):
    count = len(systems)
    eye = masks_ref[8]
    results = [eye - a * masks_ref[0] for a in systems]
    for level in range(1, 8):
        width = 1 << level
        mask = masks_ref[level]
        if width < 16:
            lefts = [dot(results[i], systems[i] * mask).astype(BF) for i in range(count)]
            fixes = [dot(lefts[i], results[i]).astype(BF) for i in range(count)]
            results = [results[i] - fixes[i] for i in range(count)]
        else:
            lefts = [dot(odd_rows(results[i], width), systems[i] * mask).astype(BF) for i in range(count)]
            fixes = [dot(lefts[i], results[i]).astype(BF) for i in range(count)]
            results = [put_odd(results[i], fixes[i], width) for i in range(count)]
    return [r - eye for r in results]


def places():
    dp = lax.axis_index("dp")
    return lax.div(dp, 4), lax.rem(lax.div(dp, 2), 2), lax.rem(dp, 2), lax.axis_index("sample")


def remote(src, dst, send, recv, where):
    return pltpu.make_async_remote_copy(
        src_ref=src, dst_ref=dst, send_sem=send, recv_sem=recv, device_id=where, device_id_type=MESH
    )


def greet(partners):
    barrier = pltpu.get_barrier_semaphore()
    for partner in partners:
        pl.semaphore_signal(barrier, inc=1, device_id=partner, device_id_type=MESH)
    pl.semaphore_wait(barrier, len(partners))


def lane_block(index, width):
    return pl.ds(pl.multiple_of(index * width, width), width)


def first_kernel(
    samples, q_ref, k_ref, v_ref, g_ref, small_ref, gain_ref, state_ref, reward_ref, cot_ref, weight_ref,
    core_ref, read_ref, weighted_ref, part_ref, all_ref,
    masks_ref, states_ref, rewards_ref, mixed_ref, other_ref, weighted_other_ref, gsend_ref, grecv_ref, acc_ref,
    st_send, st_recv, rw_send, rw_recv, wt_send, wt_recv, mx_send, mx_recv, g_send, g_recv,
    w1_send, w1_recv, w2_send, w2_recv, w3_send, w3_recv, w4_send, w4_recv, local_sem,
):
    x, yl, core_id, me = places()
    chip = x * 2 + yl
    sibling = {"dp": chip * 2 + 1 - core_id, "sample": me}

    def at_chip(index):
        return {"dp": index * 2 + core_id, "sample": me}

    def in_group(offset):
        return {"sample": lax.rem(me + offset, GROUP)}

    y_hi, z = lax.div(me, 4), lax.rem(me, 4)
    far = (1 - y_hi) * 4 + z

    def z_peer(offset):
        return {"sample": y_hi * 4 + lax.rem(z + offset, 4)}

    chip_peers = []
    for t in range(1, CHIPS):
        chip_peers.append(lax.rem(x + t // 2, 4) * 2 + lax.rem(yl + t % 2, 2))
    group_peers = [in_group(o) for o in range(1, GROUP)]
    greet([sibling] + [at_chip(c) for c in chip_peers] + group_peers)

    st_copies = [remote(state_ref, states_ref.at[me], st_send.at[o], st_recv.at[o], group_peers[o]) for o in range(GROUP - 1)]
    rw_copies = [remote(reward_ref, rewards_ref.at[me], rw_send.at[o], rw_recv.at[o], group_peers[o]) for o in range(GROUP - 1)]
    for copy in st_copies + rw_copies:
        copy.start()
    mine = all_ref.at[me, core_id, lane_block(chip, 128)]
    w1_copies = [remote(weight_ref.at[me], mine, w1_send.at[t], w1_recv.at[t], at_chip(chip_peers[t])) for t in range(CHIPS - 1)]
    for copy in w1_copies:
        copy.start()
    own = pltpu.make_async_copy(weight_ref.at[me], mine, local_sem)
    own.start()
    states_ref[me] = state_ref[...]
    rewards_ref[me] = reward_ref[...]

    held = all_ref.at[me, core_id]
    far_held = all_ref.at[far, core_id]
    w2_copy = remote(held, held, w2_send, w2_recv, {"sample": far})
    w3_copies = [remote(held, held, w3_send.at[o], w3_recv.at[o], z_peer(o + 1)) for o in range(3)]
    w3_far = [remote(far_held, far_held, w3_send.at[3 + o], w3_recv.at[3 + o], z_peer(o + 1)) for o in range(3)]

    def shared(index, slot):
        piece = all_ref.at[index, core_id]
        return remote(piece, piece, w4_send.at[slot], w4_recv.at[slot], sibling)

    def came(offset):
        return y_hi * 4 + lax.rem(z + 4 - offset, 4)

    def came_far(offset):
        return (1 - y_hi) * 4 + lax.rem(z + 4 - offset, 4)

    w4_copies = [shared(me, 0), shared(far, 1)]
    w4_copies += [shared(came(o + 1), 2 + o) for o in range(3)]
    w4_copies += [shared(came_far(o + 1), 5 + o) for o in range(3)]

    rows = iota((LEN, LEN), 0)
    cols = iota((LEN, LEN), 1)
    for level in range(8):
        same = (rows >> (level + 1)) == (cols >> (level + 1))
        below = (rows >> level) > (cols >> level)
        masks_ref[level] = jnp.where(same & below, 1.0, 0.0).astype(BF)
    masks_ref[8] = jnp.where(rows == cols, 1.0, 0.0).astype(BF)
    masks_ref[9] = jnp.where(rows <= cols, 1.0, 0.0).astype(BF)
    gain = gain_ref[...]

    def pair_at(t):
        return lax.rem(x + 3 - lax.div(t, 2), 4) * 2 + lax.rem(yl + 1 - lax.rem(t, 2), 2)

    wt_copy = remote(weighted_ref, weighted_other_ref, wt_send, wt_recv, sibling)

    def mixed_copy(t):
        return remote(mixed_ref.at[t, 1 - core_id], other_ref.at[t], mx_send.at[t], mx_recv.at[t], sibling)

    def to_row(t):
        target = lax.rem(x + 3 - lax.div(t, 2), 4) * 2 + yl
        return remote(gsend_ref.at[t], grecv_ref.at[t], g_send.at[t], g_recv.at[t], at_chip(target))

    to_column = remote(gsend_ref.at[6], grecv_ref.at[6], g_send.at[6], g_recv.at[6], at_chip(x * 2 + 1 - yl))

    def forward_step(t):
        pair = pair_at(t)
        small = small_ref[pair]
        first = small.astype(BF)
        rest = small - first.astype(F32)
        second = rest.astype(BF)
        third = (rest - second.astype(F32)).astype(BF)
        upper = masks_ref[9]
        running = dot(first, upper) + dot(second, upper) + dot(third, upper)
        by_row = jnp.where(iota(small.shape, 0) < 2 * samples, jax.nn.sigmoid(small), running)
        columns = by_row.T
        causal = rows >= cols
        strict = rows > cols
        diagonal = rows == cols
        systems, scores, rights, queries = [], [], [], []
        for s in range(samples):
            q = q_ref[s, :, lane_block(pair, 128)]
            k = k_ref[s, :, lane_block(pair, 128)]
            qk = dot(jnp.concatenate([k, q], axis=0), k, ((1,), (1,)))
            kk, qk = qk[:LEN], qk[LEN:]
            kf = k.astype(F32)
            qf = q.astype(F32)
            k_row = lax.rsqrt(jnp.sum(jnp.where(diagonal, kk, 0.0), axis=0, keepdims=True) + 1e-6)
            k_col = lax.rsqrt(jnp.sum(kf * kf, axis=1, keepdims=True) + 1e-6)
            q_col = lax.rsqrt(jnp.sum(qf * qf, axis=1, keepdims=True) + 1e-6) * (128 ** -0.5)
            kk = kk * k_row
            qk = qk * k_row
            v = v_ref[s, :, lane_block(pair, 256)].astype(F32)
            for r in range(2):
                i = 2 * s + r
                beta = columns[:, i:i + 1]
                c_col = columns[:, 2 * samples + i:2 * samples + i + 1]
                c_row = by_row[2 * samples + i:2 * samples + i + 1]
                falloff = jnp.exp(jnp.where(causal, c_col - c_row, 0.0))
                a = jnp.where(strict, falloff * kk * (beta * k_col), 0.0)
                p = jnp.where(causal, falloff * qk * q_col, 0.0)
                growth = jnp.exp(c_col)
                systems.append(a.astype(BF))
                scores.append(split(p))
                rights.append(
                    jnp.concatenate([beta * v[:, 128 * r:128 * r + 128], (beta * growth * k_col) * kf], axis=1)
                )
                queries.append((growth * q_col) * qf)
        solved = inverses(systems, masks_ref)

        @pl.when(t == 0)
        def _():
            for copy in st_copies:
                copy.wait()

        for s in range(samples):
            gates = g_ref[s, :, lane_block(pair, 256)].astype(F32)
            for r in range(2):
                i = 2 * s + r
                u = rights[i] + dot(solved[i], rights[i].astype(BF))
                u_high, u_low = split(u)
                p_high, p_low = scores[i]
                pu = dot(p_high, u_high) + (dot(p_low, u_high) + dot(p_high, u_low))
                read = (queries[i] - pu[:, 128:]).astype(BF)
                core = pu[:, :128] + dot(read, states_ref[pair, r])
                gate = gates[:, 128 * r:128 * r + 128]
                scale = lax.rsqrt(jnp.mean(core * core, axis=1, keepdims=True) + 1e-6)
                mixed_ref[t, r, pl.ds(s * LEN, LEN)] = (core * scale * gain * (gate * jax.nn.sigmoid(gate))).astype(BF)
                core_ref[pair, r, s] = core.astype(BF)
                read_ref[pair, r, s] = read
        mixed_copy(t).start()

    def partial(t):
        ours = mixed_ref[t, core_id]
        theirs = other_ref[t]
        for block in range(4):
            at = pl.ds(block * 512, 512)
            acc_ref[:, at] = dot(ours, weighted_ref[:, at], ((0,), (0,))) + dot(
                theirs, weighted_other_ref[:, at], ((0,), (0,))
            )

    def gradient_step(t):
        mixed_copy(t).wait()

        @pl.when(t == 0)
        def _():
            wt_copy.wait()

        partial(t)

        @pl.when(t < 6)
        def _():
            gsend_ref[t] = acc_ref[...].astype(BF)
            to_row(t).start()

        @pl.when(t == 6)
        def _():
            total = acc_ref[...]
            for slot in (0, 2, 4):
                to_row(slot).wait()
                total = total + grecv_ref[slot].astype(F32)
            gsend_ref[6] = total.astype(BF)
            to_column.start()

    def step(t, carry):
        forward_step(t)

        @pl.when(t == 0)
        def _():
            for copy in rw_copies:
                copy.wait()
            rewards = rewards_ref[...]
            count = GROUP * samples
            real = iota((GROUP, 8, 128), 1) < samples
            centre = jnp.sum(rewards, axis=(0, 1), keepdims=True) / count
            off = jnp.where(real, rewards - centre, 0.0)
            spread = jnp.sqrt(jnp.sum(off * off, axis=(0, 1), keepdims=True) / count)
            coefficient = ((reward_ref[...] - centre[0]) / jnp.maximum(spread[0], 0.6)) / LEN
            for s in range(samples):
                factor = coefficient[s:s + 1]
                for block in range(16):
                    at = pl.ds(block * 128, 128)
                    weighted_ref[pl.ds(s * LEN, LEN), at] = (cot_ref[s, :, at].astype(F32) * factor).astype(BF)
            wt_copy.start()

        @pl.when(t == 1)
        def _():
            own.wait()
            for copy in w1_copies:
                copy.wait()
            w2_copy.start()
            for copy in w3_copies:
                copy.start()
            w4_copies[0].start()

        @pl.when(t == 2)
        def _():
            w2_copy.wait()
            for copy in w3_far:
                copy.start()
            w4_copies[1].start()

        @pl.when(t == 6)
        def _():
            for o in range(3):
                w3_copies[o].wait()
                w4_copies[2 + o].start()

        @pl.when(t > 0)
        def _():
            gradient_step(t - 1)

        return carry

    lax.fori_loop(0, CHIPS, step, 0)
    for o in range(3):
        w3_far[o].wait()
        w4_copies[5 + o].start()
    mixed_copy(7).wait()
    partial(7)
    total = acc_ref[...]
    for slot in (1, 3, 5):
        to_row(slot).wait()
        total = total + grecv_ref[slot].astype(F32)
    to_column.wait()
    part_ref[...] = total + grecv_ref[6].astype(F32)
    for copy in w4_copies:
        copy.wait()


def first(q, k, v, g, small, gain, state, reward, cot, weight):
    samples, _, wide = v.shape
    heads = wide // 128
    pairs = heads // 2
    dma = pltpu.SemaphoreType.DMA
    vmem = pl.BlockSpec(memory_space=pltpu.VMEM)
    anywhere = pl.BlockSpec(memory_space=pl.ANY)
    tokens = samples * LEN
    return pl.pallas_call(
        functools.partial(first_kernel, samples),
        in_specs=[vmem] * 9 + [anywhere],
        out_specs=[vmem] * 4 + [anywhere],
        out_shape=[
            jax.ShapeDtypeStruct((pairs, 2, samples, LEN, 128), BF),
            jax.ShapeDtypeStruct((pairs, 2, samples, LEN, 128), BF),
            jax.ShapeDtypeStruct((tokens, wide), BF),
            jax.ShapeDtypeStruct((128, wide), F32),
            jax.ShapeDtypeStruct((GROUP, 2, wide // 2, wide // GROUP), BF),
        ],
        scratch_shapes=[
            pltpu.VMEM((10, LEN, LEN), BF),
            pltpu.VMEM((GROUP, 2, 128, 128), BF),
            pltpu.VMEM((GROUP, 8, 128), F32),
            pltpu.VMEM((pairs, 2, tokens, 128), BF),
            pltpu.VMEM((pairs, tokens, 128), BF),
            pltpu.VMEM((tokens, wide), BF),
            pltpu.VMEM((7, 128, wide), BF),
            pltpu.VMEM((7, 128, wide), BF),
            pltpu.VMEM((128, wide), F32),
            dma((7,)), dma((7,)), dma((7,)), dma((7,)), dma, dma, dma((8,)), dma((8,)), dma((7,)), dma((7,)),
            dma((7,)), dma((7,)), dma, dma, dma((6,)), dma((6,)), dma((8,)), dma((8,)), dma,
        ],
        compiler_params=pltpu.CompilerParams(
            collective_id=0, has_side_effects=True, vmem_limit_bytes=60 * 1024 * 1024
        ),
    )(q, k, v, g, small, gain, state, reward, cot, weight)


def second_kernel(
    samples, weighted_ref, g_ref, core_ref, read_ref, gain_ref, part_ref, all_ref,
    prefix_ref, grad_ref,
    pieces_ref, psend_ref, precv_ref, slices_ref, sum_ref,
    load_sem, p_send, p_recv, s_send, s_recv, a_send, a_recv,
):
    me = lax.axis_index("sample")

    def in_group(offset):
        return {"sample": lax.rem(me + offset, GROUP)}

    def load(u):
        pair = lax.rem(me + 1 + u, GROUP)
        return pltpu.make_async_copy(
            all_ref.at[:, :, lane_block(pair, 128)], pieces_ref.at[lax.rem(u, 2)], load_sem.at[lax.rem(u, 2)]
        )

    load(0).start()
    greet([in_group(o) for o in range(1, GROUP)])
    height = 128 // GROUP

    def slab(index):
        return pl.ds(pl.multiple_of(index * height, height), height)

    s_copies = [
        remote(part_ref.at[slab(lax.rem(me + o, GROUP))], slices_ref.at[o - 1], s_send.at[o - 1], s_recv.at[o - 1], in_group(o))
        for o in range(1, GROUP)
    ]
    for copy in s_copies:
        copy.start()
    a_copies = [
        remote(sum_ref, grad_ref.at[slab(me)], a_send.at[o - 1], a_recv.at[o - 1], in_group(o))
        for o in range(1, GROUP)
    ]
    gain = gain_ref[...]

    def prefix_copy(u):
        return remote(psend_ref.at[u], precv_ref.at[u], p_send.at[u], p_recv.at[u], in_group(u + 1))

    def pair_grads(u):
        pair = lax.rem(me + 1 + u, GROUP)
        load(u).wait()
        slot = lax.rem(u, 2)
        back = jnp.zeros((weighted_ref.shape[0], 256), F32)
        for block in range(GROUP):
            piece = pieces_ref[slot, block].reshape(256, 256)
            back = back + dot(weighted_ref[:, block * 256:block * 256 + 256], piece, ((1,), (1,)))
        grads = [jnp.zeros((128, 128), F32), jnp.zeros((128, 128), F32)]
        for s in range(samples):
            gates = g_ref[s, :, lane_block(pair, 256)].astype(F32)
            for r in range(2):
                core = core_ref[pair, r, s].astype(F32)
                gate = gates[:, 128 * r:128 * r + 128]
                scale = lax.rsqrt(jnp.mean(core * core, axis=1, keepdims=True) + 1e-6)
                normed = core * scale
                lifted = back[s * LEN:s * LEN + LEN, 128 * r:128 * r + 128] * gain * (gate * jax.nn.sigmoid(gate))
                core_grad = scale * (lifted - normed * jnp.mean(lifted * normed, axis=1, keepdims=True))
                grads[r] = grads[r] + dot(read_ref[pair, r, s], core_grad.astype(BF), ((0,), (0,)))
        return grads

    def step(u, carry):
        load(u + 1).start()
        grads = pair_grads(u)
        psend_ref[u, 0] = grads[0]
        psend_ref[u, 1] = grads[1]
        prefix_copy(u).start()

        @pl.when(u == 3)
        def _():
            total = part_ref[slab(me)]
            for o in range(GROUP - 1):
                s_copies[o].wait()
                total = total + slices_ref[o]
            sum_ref[...] = total
            grad_ref[slab(me)] = total
            for copy in a_copies:
                copy.start()

        return carry

    lax.fori_loop(0, GROUP - 1, step, 0)
    own = pair_grads(GROUP - 1)
    for u in range(GROUP - 1):
        prefix_copy(u).wait()
    for r in range(2):
        total = own[r]
        for u in range(GROUP - 1):
            total = total + precv_ref[u, r].astype(F32)
        prefix_ref[r] = total
    for copy in a_copies:
        copy.wait()


def second(weighted, g, core, read, gain, part, whole):
    samples, _, wide = g.shape
    dma = pltpu.SemaphoreType.DMA
    vmem = pl.BlockSpec(memory_space=pltpu.VMEM)
    return pl.pallas_call(
        functools.partial(second_kernel, samples),
        in_specs=[vmem] * 6 + [pl.BlockSpec(memory_space=pl.ANY)],
        out_specs=[vmem] * 2,
        out_shape=[
            jax.ShapeDtypeStruct((2, 128, 128), F32),
            jax.ShapeDtypeStruct((128, wide), F32),
        ],
        scratch_shapes=[
            pltpu.VMEM((2, GROUP, 2, 128, wide // GROUP), BF),
            pltpu.VMEM((7, 2, 128, 128), F32),
            pltpu.VMEM((7, 2, 128, 128), F32),
            pltpu.VMEM((7, 128 // GROUP, wide), F32),
            pltpu.VMEM((128 // GROUP, wide), F32),
            dma((2,)), dma((7,)), dma((7,)), dma((7,)), dma((7,)), dma((7,)), dma((7,)),
        ],
        compiler_params=pltpu.CompilerParams(
            collective_id=1, has_side_effects=True, vmem_limit_bytes=60 * 1024 * 1024
        ),
    )(weighted, g, core, read, gain, part, whole)


def adam_update(weight, first_moment, second_moment, gradient):
    first_new = 0.9 * first_moment + 0.1 * gradient
    second_new = 0.95 * second_moment + 0.05 * gradient * gradient
    direction = first_new / (1.0 - 0.9**10) / (jnp.sqrt(second_new / (1.0 - 0.95**10)) + 1e-08)
    weight_new = weight - 0.001 * (direction + 0.1 * weight)
    return (weight_new, first_new, second_new)


def local(
    query_vectors,
    key_vectors,
    value_vectors,
    output_gates,
    beta_logits,
    decay_logits,
    decay_rates,
    norm_gain,
    prefix_states,
    cotangent,
    rewards,
    out_weight,
    first_moment,
    second_moment,
):
    samples = rewards.shape[1]
    heads = beta_logits.shape[2]
    rows, wide = out_weight.shape
    weight16 = out_weight.astype(BF).reshape(rows, GROUP, wide // GROUP).transpose(1, 0, 2)
    decays = -decay_rates[:, None] * jax.nn.softplus(decay_logits[0].astype(F32))

    def by_pair(source):
        return source.reshape(samples, heads // 2, 2, LEN).transpose(1, 0, 2, 3).reshape(heads // 2, 2 * samples, LEN)

    small = jnp.concatenate([by_pair(beta_logits[0].astype(F32)), by_pair(decays)], axis=1)
    gain = norm_gain[None]
    gates = output_gates[0]
    reward_tile = jnp.broadcast_to(jnp.pad(rewards[0], (0, 8 - samples))[:, None], (8, 128))
    core, read, weighted, part, whole = first(
        query_vectors[0], key_vectors[0], value_vectors[0], gates, small, gain,
        prefix_states[0].astype(BF), reward_tile, cotangent[0], weight16,
    )
    prefix_grad, gradient = second(weighted, gates, core, read, gain, part, whole)
    return (prefix_grad[None],) + adam_update(out_weight, first_moment, second_moment, gradient)


def solution(mesh):
    placed = (
        P("dp", "sample", None, None),
        P("dp", "sample", None, None),
        P("dp", "sample", None, None),
        P("dp", "sample", None, None),
        P("dp", "sample", None, None),
        P("dp", "sample", None, None),
        P(),
        P(),
        P("dp", "sample", None, None),
        P("dp", "sample", None, None),
        P("dp", "sample"),
        P("dp", None),
        P("dp", None),
        P("dp", None),
    )
    return jax.shard_map(
        local,
        mesh=mesh,
        in_specs=placed,
        out_specs=(P("dp", "sample", None, None), P("dp", None), P("dp", None), P("dp", None)),
        check_vma=False,
    )
```

```python
import functools
import jax
import jax.numpy as jnp
from jax import lax
from jax.experimental import pallas as pl
from jax.experimental.pallas import tpu as pltpu
from jax.sharding import PartitionSpec as P

LEN = 256
F32 = jnp.float32
BF = jnp.bfloat16
MESH = pl.DeviceIdType.MESH
CHIPS = 8
GROUP = 8


def dot(a, b, dims=((1,), (0,))):
    return lax.dot_general(a, b, (dims, ((), ())), preferred_element_type=F32)


def iota(shape, dim):
    return lax.broadcasted_iota(jnp.int32, shape, dim)


def split(x):
    high = x.astype(BF)
    return high, (x - high.astype(F32)).astype(BF)


def odd_rows(x, width):
    n = x.shape[0] // (2 * width)
    return x.reshape((n, 2, width) + x.shape[1:])[:, 1].reshape((n * width,) + x.shape[1:])


def put_odd(x, rows, width):
    n = x.shape[0] // (2 * width)
    parted = x.reshape((n, 2, width) + x.shape[1:])
    rows = rows.reshape((n, width) + x.shape[1:])
    return jnp.stack([parted[:, 0], parted[:, 1] - rows], axis=1).reshape(x.shape)


def inverses(systems, masks_ref):
    count = len(systems)
    eye = masks_ref[8]
    results = [eye - a * masks_ref[0] for a in systems]
    for level in range(1, 8):
        width = 1 << level
        mask = masks_ref[level]
        if width < 16:
            lefts = [dot(results[i], systems[i] * mask).astype(BF) for i in range(count)]
            fixes = [dot(lefts[i], results[i]).astype(BF) for i in range(count)]
            results = [results[i] - fixes[i] for i in range(count)]
        else:
            lefts = [dot(odd_rows(results[i], width), systems[i] * mask).astype(BF) for i in range(count)]
            fixes = [dot(lefts[i], results[i]).astype(BF) for i in range(count)]
            results = [put_odd(results[i], fixes[i], width) for i in range(count)]
    return [r - eye for r in results]


def places():
    dp = lax.axis_index("dp")
    return lax.div(dp, 4), lax.rem(lax.div(dp, 2), 2), lax.rem(dp, 2), lax.axis_index("sample")


def remote(src, dst, send, recv, where):
    return pltpu.make_async_remote_copy(
        src_ref=src, dst_ref=dst, send_sem=send, recv_sem=recv, device_id=where, device_id_type=MESH
    )


def lane_block(index, width):
    return pl.ds(pl.multiple_of(index * width, width), width)


def whole_kernel(
    samples, rate_ref, reward_ref, gain_ref, beta_ref, decay_ref, state_ref, weight_ref,
    q_in, k_in, v_in, g_in, cot_in,
    prefix_ref, grad_ref,
    q_ref, k_ref, v_ref, g_ref, cot_ref,
    masks_ref, small_ref, states_ref, rewards_ref, tile_ref, mixed_ref, other_ref, weighted_ref, weighted_other_ref,
    core_ref, read_ref, all_ref, gsend_ref, grecv_ref, acc_ref, part_ref, slices_ref, sum_ref, psend_ref, precv_ref,
    in_sem, st_send, st_recv, rw_send, rw_recv, wt_send, wt_recv, mx_send, mx_recv, g_send, g_recv,
    w1_send, w1_recv, w2_send, w2_recv, w3_send, w3_recv, w4_send, w4_recv,
    s_send, s_recv, a_send, a_recv, p_send, p_recv,
):
    loads = [
        pltpu.make_async_copy(source, target, in_sem.at[i])
        for i, (source, target) in enumerate(
            ((k_in, k_ref), (q_in, q_ref), (v_in, v_ref), (g_in, g_ref), (cot_in, cot_ref))
        )
    ]
    for copy in loads:
        copy.start()
    x, yl, core_id, me = places()
    chip = x * 2 + yl
    y_hi, z = lax.div(me, 4), lax.rem(me, 4)
    far = (1 - y_hi) * 4 + z
    sibling = {"dp": chip * 2 + 1 - core_id, "sample": me}
    column = {"dp": (x * 2 + 1 - yl) * 2 + core_id, "sample": me}

    def at_chip(index):
        return {"dp": index * 2 + core_id, "sample": me}

    def in_group(offset):
        return {"sample": lax.rem(me + offset, GROUP)}

    def along_z(offset):
        return y_hi * 4 + lax.rem(z + offset, 4)

    def far_along_z(offset):
        return (1 - y_hi) * 4 + lax.rem(z + offset, 4)

    chip_peers = [lax.rem(x + t // 2, 4) * 2 + lax.rem(yl + t % 2, 2) for t in range(1, CHIPS)]
    group_peers = [in_group(o) for o in range(1, GROUP)]
    others = [sibling] + [at_chip(c) for c in chip_peers] + group_peers
    barrier = pltpu.get_barrier_semaphore()
    for partner in others:
        pl.semaphore_signal(barrier, inc=1, device_id=partner, device_id_type=MESH)

    states_ref[me] = state_ref[...].astype(BF)
    mine = all_ref.at[me, core_id, lane_block(chip, 128)]
    mine[...] = weight_ref[:, lane_block(me, 256)].astype(BF)
    tile_row = iota((8, 128), 0)
    tile = jnp.zeros((8, 128), F32)
    for s in range(samples):
        tile = jnp.where(tile_row == s, reward_ref[0, s], tile)
    tile_ref[...] = tile
    rewards_ref[me] = tile
    for s in range(samples):
        betas = beta_ref[s].astype(F32)
        softs = jax.nn.softplus(decay_ref[s].astype(F32))
        for pair in range(betas.shape[0] // 2):
            small_ref[pair, 2 * s:2 * s + 2] = betas[2 * pair:2 * pair + 2]
            small_ref[pair, 2 * (samples + s):2 * (samples + s) + 2] = softs[2 * pair:2 * pair + 2]
    rows = iota((LEN, LEN), 0)
    cols = iota((LEN, LEN), 1)
    for level in range(8):
        same = (rows >> (level + 1)) == (cols >> (level + 1))
        below = (rows >> level) > (cols >> level)
        masks_ref[level] = jnp.where(same & below, 1.0, 0.0).astype(BF)
    masks_ref[8] = jnp.where(rows == cols, 1.0, 0.0).astype(BF)
    masks_ref[9] = jnp.where(rows <= cols, 1.0, 0.0).astype(BF)
    gain = gain_ref[...]
    pl.semaphore_wait(barrier, len(others))

    st_copies = [
        remote(states_ref.at[me], states_ref.at[me], st_send.at[o], st_recv.at[o], group_peers[o])
        for o in range(GROUP - 1)
    ]
    rw_copies = [
        remote(tile_ref, rewards_ref.at[me], rw_send.at[o], rw_recv.at[o], group_peers[o]) for o in range(GROUP - 1)
    ]
    w1_copies = [
        remote(mine, mine, w1_send.at[t], w1_recv.at[t], at_chip(chip_peers[t])) for t in range(CHIPS - 1)
    ]
    for copy in st_copies + rw_copies + w1_copies:
        copy.start()

    held = all_ref.at[me, core_id]
    far_held = all_ref.at[far, core_id]
    w2_copy = remote(held, held, w2_send, w2_recv, {"sample": far})
    w3_near = [
        remote(held, held, w3_send.at[i], w3_recv.at[i], {"sample": along_z(o)}) for i, o in ((0, 1), (1, 3))
    ]
    w3_far = [
        remote(far_held, far_held, w3_send.at[i], w3_recv.at[i], {"sample": along_z(o)}) for i, o in ((2, 1), (3, 3))
    ]

    def passed(index, half, slot, offset):
        piece = all_ref.at[index, core_id, pl.ds(half * 512, 512)]
        return remote(piece, piece, w3_send.at[slot], w3_recv.at[slot], {"sample": along_z(offset)})

    w3_near_on = [passed(along_z(3), 0, 4, 1), passed(along_z(1), 1, 5, 3)]
    w3_far_on = [passed(far_along_z(3), 0, 6, 1), passed(far_along_z(1), 1, 7, 3)]

    def shared(index, slot):
        piece = all_ref.at[index, core_id]
        return remote(piece, piece, w4_send.at[slot], w4_recv.at[slot], sibling)

    w4_copies = [shared(me, 0), shared(far, 1)]
    w4_copies += [shared(along_z(1), 2), shared(along_z(3), 3), shared(far_along_z(1), 4), shared(far_along_z(3), 5)]
    w4_copies += [shared(along_z(2), 6), shared(far_along_z(2), 7)]

    def shift_at(t):
        u = lax.div(t, 2)
        return 2 - u + 3 * lax.div(u, 2) - 2 * lax.div(u, 3)

    def pair_at(t):
        return lax.rem(x + shift_at(t), 4) * 2 + lax.rem(yl + 1 - lax.rem(t, 2), 2)

    wt_copy = remote(weighted_ref, weighted_other_ref, wt_send, wt_recv, sibling)

    def mixed_copy(t):
        return remote(mixed_ref.at[t, 1 - core_id], other_ref.at[t], mx_send.at[t], mx_recv.at[t], sibling)

    def to_row(t):
        target = lax.rem(x + shift_at(t), 4) * 2 + yl
        return remote(gsend_ref.at[t], grecv_ref.at[t], g_send.at[t], g_recv.at[t], at_chip(target))

    def to_column(t):
        return remote(gsend_ref.at[t], grecv_ref.at[t], g_send.at[t], g_recv.at[t], column)

    def forward_step(t):
        pair = pair_at(t)
        raw = small_ref[pair]
        raw_row = iota(raw.shape, 0)
        rate = jnp.where(lax.rem(raw_row, 2) == 0, rate_ref[2 * pair], rate_ref[2 * pair + 1])
        small = raw * -rate
        first = small.astype(BF)
        rest = small - first.astype(F32)
        second = rest.astype(BF)
        third = (rest - second.astype(F32)).astype(BF)
        upper = masks_ref[9]
        running = dot(first, upper) + dot(second, upper) + dot(third, upper)
        by_row = jnp.where(raw_row < 2 * samples, jax.nn.sigmoid(raw), running)
        columns = by_row.T
        causal = rows >= cols
        strict = rows > cols
        diagonal = rows == cols
        systems, scores, rights, queries = [], [], [], []
        for s in range(samples):
            q = q_ref[s, :, lane_block(pair, 128)]
            k = k_ref[s, :, lane_block(pair, 128)]
            qk = dot(jnp.concatenate([k, q], axis=0), k, ((1,), (1,)))
            kk, qk = qk[:LEN], qk[LEN:]
            kf = k.astype(F32)
            qf = q.astype(F32)
            k_row = lax.rsqrt(jnp.sum(jnp.where(diagonal, kk, 0.0), axis=0, keepdims=True) + 1e-6)
            k_col = lax.rsqrt(jnp.sum(kf * kf, axis=1, keepdims=True) + 1e-6)
            q_col = lax.rsqrt(jnp.sum(qf * qf, axis=1, keepdims=True) + 1e-6) * (128 ** -0.5)
            kk = kk * k_row
            qk = qk * k_row
            v = v_ref[s, :, lane_block(pair, 256)].astype(F32)
            for r in range(2):
                i = 2 * s + r
                beta = columns[:, i:i + 1]
                c_col = columns[:, 2 * samples + i:2 * samples + i + 1]
                c_row = by_row[2 * samples + i:2 * samples + i + 1]
                falloff = jnp.exp(jnp.where(causal, c_col - c_row, 0.0))
                a = jnp.where(strict, falloff * kk * (beta * k_col), 0.0)
                p = jnp.where(causal, falloff * qk * q_col, 0.0)
                growth = jnp.exp(c_col)
                systems.append(a.astype(BF))
                scores.append(split(p))
                rights.append(
                    jnp.concatenate([beta * v[:, 128 * r:128 * r + 128], (beta * growth * k_col) * kf], axis=1)
                )
                queries.append((growth * q_col) * qf)
        solved = inverses(systems, masks_ref)

        @pl.when(t == 0)
        def _():
            for copy in st_copies:
                copy.wait()

        for s in range(samples):
            gates = g_ref[s, :, lane_block(pair, 256)].astype(F32)
            for r in range(2):
                i = 2 * s + r
                u = rights[i] + dot(solved[i], rights[i].astype(BF))
                u_high, u_low = split(u)
                p_high, p_low = scores[i]
                pu = dot(p_high, u_high) + (dot(p_low, u_high) + dot(p_high, u_low))
                read = (queries[i] - pu[:, 128:]).astype(BF)
                core = pu[:, :128] + dot(read, states_ref[pair, r])
                gate = gates[:, 128 * r:128 * r + 128]
                scale = lax.rsqrt(jnp.mean(core * core, axis=1, keepdims=True) + 1e-6)
                mixed_ref[t, r, pl.ds(s * LEN, LEN)] = (core * scale * gain * (gate * jax.nn.sigmoid(gate))).astype(BF)
                core_ref[pair, r, s] = core.astype(BF)
                read_ref[pair, r, s] = read
        mixed_copy(t).start()

    def weigh():
        for copy in rw_copies:
            copy.wait()
        rewards = rewards_ref[...]
        count = GROUP * samples
        real = iota((GROUP, 8, 128), 1) < samples
        centre = jnp.sum(rewards, axis=(0, 1), keepdims=True) / count
        off = jnp.where(real, rewards - centre, 0.0)
        spread = jnp.sqrt(jnp.sum(off * off, axis=(0, 1), keepdims=True) / count)
        coefficient = ((tile_ref[...] - centre[0]) / jnp.maximum(spread[0], 0.6)) / LEN
        for s in range(samples):
            factor = coefficient[s:s + 1]
            for block in range(16):
                at = pl.ds(block * 128, 128)
                weighted_ref[pl.ds(s * LEN, LEN), at] = (cot_ref[s, :, at].astype(F32) * factor).astype(BF)
        wt_copy.start()

    def partial(t):
        ours = mixed_ref[t, core_id]
        theirs = other_ref[t]
        for block in range(4):
            at = pl.ds(block * 512, 512)
            acc_ref[:, at] = dot(ours, weighted_ref[:, at], ((0,), (0,))) + dot(
                theirs, weighted_other_ref[:, at], ((0,), (0,))
            )

    def gradient_step(t):
        mixed_copy(t).wait()

        @pl.when(t == 0)
        def _():
            wt_copy.wait()

        partial(t)

        @pl.when(t == 0)
        def _():
            gsend_ref[0] = acc_ref[...].astype(BF)
            to_column(0).start()

        @pl.when(t == 1)
        def _():
            to_column(0).wait()
            gsend_ref[1] = (acc_ref[...] + grecv_ref[0].astype(F32)).astype(BF)
            to_row(1).start()

        @pl.when((t > 1) & (t < 6))
        def _():
            gsend_ref[t] = acc_ref[...].astype(BF)
            to_row(t).start()

        @pl.when(t == 6)
        def _():
            total = acc_ref[...]
            for slot in (2, 4):
                to_row(slot).wait()
                total = total + grecv_ref[slot].astype(F32)
            gsend_ref[6] = total.astype(BF)
            to_column(6).start()

    for copy in loads:
        copy.wait()

    def step(t, carry):
        forward_step(t)

        @pl.when(t == 0)
        def _():
            weigh()

        @pl.when(t == 1)
        def _():
            for copy in w1_copies:
                copy.wait()
            w2_copy.start()
            for copy in w3_near:
                copy.start()
            w4_copies[0].start()

        @pl.when(t == 2)
        def _():
            w2_copy.wait()
            for copy in w3_far:
                copy.start()
            w4_copies[1].start()

        @pl.when(t == 3)
        def _():
            for copy in w3_near:
                copy.wait()
            for copy in w3_near_on:
                copy.start()
            w4_copies[2].start()
            w4_copies[3].start()

        @pl.when(t == 5)
        def _():
            for copy in w3_far:
                copy.wait()
            for copy in w3_far_on:
                copy.start()
            w4_copies[4].start()
            w4_copies[5].start()

        @pl.when(t == 6)
        def _():
            for copy in w3_near_on:
                copy.wait()
            w4_copies[6].start()

        @pl.when(t > 0)
        def _():
            gradient_step(t - 1)

        return carry

    lax.fori_loop(0, CHIPS, step, 0)
    for copy in w3_far_on:
        copy.wait()
    w4_copies[7].start()
    mixed_copy(7).wait()
    partial(7)
    total = acc_ref[...]
    for slot in (1, 3, 5):
        to_row(slot).wait()
        total = total + grecv_ref[slot].astype(F32)
    to_column(6).wait()
    total = total + grecv_ref[6].astype(F32)
    acc_ref[...] = total
    part_ref[...] = total.astype(BF)

    height = 128 // GROUP

    def slab(index):
        return pl.ds(pl.multiple_of(index * height, height), height)

    s_copies = [
        remote(
            part_ref.at[slab(lax.rem(me + o, GROUP))], slices_ref.at[o - 1], s_send.at[o - 1], s_recv.at[o - 1], in_group(o)
        )
        for o in range(1, GROUP)
    ]
    for copy in s_copies:
        copy.start()
    a_copies = [
        remote(sum_ref, grad_ref.at[slab(me)], a_send.at[o - 1], a_recv.at[o - 1], in_group(o))
        for o in range(1, GROUP)
    ]
    for copy in w4_copies:
        copy.wait()

    def prefix_copy(u):
        return remote(psend_ref.at[u], precv_ref.at[u], p_send.at[u], p_recv.at[u], in_group(u + 1))

    def pair_grads(u):
        pair = lax.rem(me + 1 + u, GROUP)
        back = jnp.zeros((weighted_ref.shape[0], 256), F32)
        for block in range(GROUP):
            piece = all_ref[block, :, lane_block(pair, 128)].reshape(256, 256)
            back = back + dot(weighted_ref[:, block * 256:block * 256 + 256], piece, ((1,), (1,)))
        grads = [jnp.zeros((128, 128), F32), jnp.zeros((128, 128), F32)]
        for s in range(samples):
            gates = g_ref[s, :, lane_block(pair, 256)].astype(F32)
            for r in range(2):
                core = core_ref[pair, r, s].astype(F32)
                gate = gates[:, 128 * r:128 * r + 128]
                scale = lax.rsqrt(jnp.mean(core * core, axis=1, keepdims=True) + 1e-6)
                normed = core * scale
                lifted = back[s * LEN:s * LEN + LEN, 128 * r:128 * r + 128] * gain * (gate * jax.nn.sigmoid(gate))
                core_grad = scale * (lifted - normed * jnp.mean(lifted * normed, axis=1, keepdims=True))
                high, low = split(core_grad)
                read = read_ref[pair, r, s]
                grads[r] = grads[r] + dot(read, high, ((0,), (0,))) + dot(read, low, ((0,), (0,)))
        return grads

    def back_step(u, carry):
        grads = pair_grads(u)
        psend_ref[u, 0] = grads[0].astype(BF)
        psend_ref[u, 1] = grads[1].astype(BF)
        prefix_copy(u).start()

        @pl.when(u == 2)
        def _():
            total = acc_ref[slab(me)]
            for o in range(GROUP - 1):
                s_copies[o].wait()
                total = total + slices_ref[o].astype(F32)
            sum_ref[...] = total
            grad_ref[slab(me)] = total
            for copy in a_copies:
                copy.start()

        return carry

    lax.fori_loop(0, GROUP - 1, back_step, 0)
    own = pair_grads(GROUP - 1)
    for u in range(GROUP - 1):
        prefix_copy(u).wait()
    for r in range(2):
        total = own[r]
        for u in range(GROUP - 1):
            total = total + precv_ref[u, r].astype(F32)
        prefix_ref[r] = total
    for copy in a_copies:
        copy.wait()


def whole(rates, rewards, gain, beta, decay, state, weight, q, k, v, g, cot):
    samples, _, wide = v.shape
    pairs = wide // 256
    tokens = samples * LEN
    dma = pltpu.SemaphoreType.DMA
    vmem = pl.BlockSpec(memory_space=pltpu.VMEM)
    smem = pl.BlockSpec(memory_space=pltpu.SMEM)
    anywhere = pl.BlockSpec(memory_space=pl.ANY)
    sems = [dma((5,))]
    for count in (7, 7, None, 8, 7, 7, None, 8, 8, 7, 7, 7):
        sems += [dma if count is None else dma((count,))] * 2
    return pl.pallas_call(
        functools.partial(whole_kernel, samples),
        in_specs=[smem, smem] + [vmem] * 5 + [anywhere] * 5,
        out_specs=[vmem] * 2,
        out_shape=[
            jax.ShapeDtypeStruct((2, 128, 128), F32),
            jax.ShapeDtypeStruct((128, wide), F32),
        ],
        scratch_shapes=[
            pltpu.VMEM(q.shape, BF),
            pltpu.VMEM(k.shape, BF),
            pltpu.VMEM(v.shape, BF),
            pltpu.VMEM(g.shape, BF),
            pltpu.VMEM(cot.shape, BF),
            pltpu.VMEM((10, LEN, LEN), BF),
            pltpu.VMEM((pairs, 4 * samples, LEN), F32),
            pltpu.VMEM((GROUP, 2, 128, 128), BF),
            pltpu.VMEM((GROUP, 8, 128), F32),
            pltpu.VMEM((8, 128), F32),
            pltpu.VMEM((pairs, 2, tokens, 128), BF),
            pltpu.VMEM((pairs, tokens, 128), BF),
            pltpu.VMEM((tokens, wide), BF),
            pltpu.VMEM((tokens, wide), BF),
            pltpu.VMEM((pairs, 2, samples, LEN, 128), BF),
            pltpu.VMEM((pairs, 2, samples, LEN, 128), BF),
            pltpu.VMEM((GROUP, 2, wide // 2, wide // GROUP), BF),
            pltpu.VMEM((7, 128, wide), BF),
            pltpu.VMEM((7, 128, wide), BF),
            pltpu.VMEM((128, wide), F32),
            pltpu.VMEM((128, wide), BF),
            pltpu.VMEM((7, 128 // GROUP, wide), BF),
            pltpu.VMEM((128 // GROUP, wide), F32),
            pltpu.VMEM((7, 2, 128, 128), BF),
            pltpu.VMEM((7, 2, 128, 128), BF),
        ] + sems,
        compiler_params=pltpu.CompilerParams(
            collective_id=0, has_side_effects=True, vmem_limit_bytes=62 * 1024 * 1024
        ),
    )(rates, rewards, gain, beta, decay, state, weight, q, k, v, g, cot)


def adam_update(weight, first_moment, second_moment, gradient):
    first_new = 0.9 * first_moment + 0.1 * gradient
    second_new = 0.95 * second_moment + 0.05 * gradient * gradient
    direction = first_new / (1.0 - 0.9**10) / (jnp.sqrt(second_new / (1.0 - 0.95**10)) + 1e-08)
    weight_new = weight - 0.001 * (direction + 0.1 * weight)
    return (weight_new, first_new, second_new)


def local(
    query_vectors,
    key_vectors,
    value_vectors,
    output_gates,
    beta_logits,
    decay_logits,
    decay_rates,
    norm_gain,
    prefix_states,
    cotangent,
    rewards,
    out_weight,
    first_moment,
    second_moment,
):
    prefix_grad, gradient = whole(
        decay_rates, rewards, norm_gain[None], beta_logits[0], decay_logits[0], prefix_states[0], out_weight,
        query_vectors[0], key_vectors[0], value_vectors[0], output_gates[0], cotangent[0],
    )
    return (prefix_grad[None],) + adam_update(out_weight, first_moment, second_moment, gradient)


def solution(mesh):
    placed = (
        P("dp", "sample", None, None),
        P("dp", "sample", None, None),
        P("dp", "sample", None, None),
        P("dp", "sample", None, None),
        P("dp", "sample", None, None),
        P("dp", "sample", None, None),
        P(),
        P(),
        P("dp", "sample", None, None),
        P("dp", "sample", None, None),
        P("dp", "sample"),
        P("dp", None),
        P("dp", None),
        P("dp", None),
    )
    return jax.shard_map(
        local,
        mesh=mesh,
        in_specs=placed,
        out_specs=(P("dp", "sample", None, None), P("dp", None), P("dp", None), P("dp", None)),
        check_vma=False,
    )
```

```python
import functools
import jax
import jax.numpy as jnp
from jax import lax
from jax.experimental import pallas as pl
from jax.experimental.pallas import tpu as pltpu
from jax.sharding import PartitionSpec as P

LEN = 256
HALF = 128
F32 = jnp.float32
BF = jnp.bfloat16
MESH = pl.DeviceIdType.MESH
CHIPS = 8
GROUP = 8


def dot(a, b, dims=((1,), (0,))):
    return lax.dot_general(a, b, (dims, ((), ())), preferred_element_type=F32)


def iota(shape, dim):
    return lax.broadcasted_iota(jnp.int32, shape, dim)


def split(x):
    high = x.astype(BF)
    return high, (x - high.astype(F32)).astype(BF)


def odd_rows(x, width):
    n = x.shape[0] // (2 * width)
    return x.reshape((n, 2, width) + x.shape[1:])[:, 1].reshape((n * width,) + x.shape[1:])


def put_odd(x, rows, width):
    n = x.shape[0] // (2 * width)
    parted = x.reshape((n, 2, width) + x.shape[1:])
    rows = rows.reshape((n, width) + x.shape[1:])
    return jnp.stack([parted[:, 0], parted[:, 1] - rows], axis=1).reshape(x.shape)


def inverses(systems, masks_ref):
    count = len(systems)
    eye = masks_ref[7]
    results = [eye - a * masks_ref[0] for a in systems]
    for level in range(1, 7):
        width = 1 << level
        mask = masks_ref[level]
        if width < 16:
            lefts = [dot(results[i], systems[i] * mask).astype(BF) for i in range(count)]
            fixes = [dot(lefts[i], results[i]).astype(BF) for i in range(count)]
            results = [results[i] - fixes[i] for i in range(count)]
        else:
            lefts = [dot(odd_rows(results[i], width), systems[i] * mask).astype(BF) for i in range(count)]
            fixes = [dot(lefts[i], results[i]).astype(BF) for i in range(count)]
            results = [put_odd(results[i], fixes[i], width) for i in range(count)]
    return [r - eye for r in results]


def places():
    dp = lax.axis_index("dp")
    return lax.div(dp, 4), lax.rem(lax.div(dp, 2), 2), lax.rem(dp, 2), lax.axis_index("sample")


def remote(src, dst, send, recv, where):
    return pltpu.make_async_remote_copy(
        src_ref=src, dst_ref=dst, send_sem=send, recv_sem=recv, device_id=where, device_id_type=MESH
    )


def lane_block(index, width):
    return pl.ds(pl.multiple_of(index * width, width), width)


def whole_kernel(
    samples, rate_ref, reward_ref, gain_ref, beta_ref, decay_ref, state_ref, weight_ref,
    q_in, k_in, v_in, g_in, cot_in,
    prefix_ref, grad_ref,
    q_ref, k_ref, v_ref, g_ref, cot_ref,
    masks_ref, upper_ref, small_ref, states_ref, rewards_ref, tile_ref, mixed_ref, other_ref, weighted_ref, weighted_other_ref,
    core_ref, read_ref, all_ref, gsend_ref, grecv_ref, acc_ref, part_ref, slices_ref, sum_ref, psend_ref, precv_ref,
    in_sem, st_send, st_recv, rw_send, rw_recv, wt_send, wt_recv, mx_send, mx_recv, g_send, g_recv,
    w1_send, w1_recv, w2_send, w2_recv, w3_send, w3_recv, w4_send, w4_recv,
    s_send, s_recv, a_send, a_recv, p_send, p_recv,
):
    loads = [
        pltpu.make_async_copy(source, target, in_sem.at[i])
        for i, (source, target) in enumerate(
            ((k_in, k_ref), (q_in, q_ref), (v_in, v_ref), (g_in, g_ref), (cot_in, cot_ref))
        )
    ]
    for copy in loads:
        copy.start()
    x, yl, core_id, me = places()
    chip = x * 2 + yl
    y_hi, z = lax.div(me, 4), lax.rem(me, 4)
    far = (1 - y_hi) * 4 + z
    sibling = {"dp": chip * 2 + 1 - core_id, "sample": me}
    column = {"dp": (x * 2 + 1 - yl) * 2 + core_id, "sample": me}

    def at_chip(index):
        return {"dp": index * 2 + core_id, "sample": me}

    def in_group(offset):
        return {"sample": lax.rem(me + offset, GROUP)}

    def along_z(offset):
        return y_hi * 4 + lax.rem(z + offset, 4)

    def far_along_z(offset):
        return (1 - y_hi) * 4 + lax.rem(z + offset, 4)

    chip_peers = [lax.rem(x + t // 2, 4) * 2 + lax.rem(yl + t % 2, 2) for t in range(1, CHIPS)]
    group_peers = [in_group(o) for o in range(1, GROUP)]
    others = [sibling] + [at_chip(c) for c in chip_peers] + group_peers
    barrier = pltpu.get_barrier_semaphore()
    for partner in others:
        pl.semaphore_signal(barrier, inc=1, device_id=partner, device_id_type=MESH)

    states_ref[me] = state_ref[...].astype(BF)
    mine = all_ref.at[me, core_id, lane_block(chip, 128)]
    mine[...] = weight_ref[:, lane_block(me, 256)].astype(BF)
    tile_row = iota((8, 128), 0)
    tile = jnp.zeros((8, 128), F32)
    for s in range(samples):
        tile = jnp.where(tile_row == s, reward_ref[0, s], tile)
    tile_ref[...] = tile
    rewards_ref[me] = tile
    for s in range(samples):
        betas = beta_ref[s].astype(F32)
        softs = jax.nn.softplus(decay_ref[s].astype(F32))
        for pair in range(betas.shape[0] // 2):
            small_ref[pair, 2 * s:2 * s + 2] = betas[2 * pair:2 * pair + 2]
            small_ref[pair, 2 * (samples + s):2 * (samples + s) + 2] = softs[2 * pair:2 * pair + 2]
    upper_ref[...] = jnp.where(iota((LEN, LEN), 0) <= iota((LEN, LEN), 1), 1.0, 0.0).astype(BF)
    rows = iota((HALF, HALF), 0)
    cols = iota((HALF, HALF), 1)
    for level in range(7):
        same = (rows >> (level + 1)) == (cols >> (level + 1))
        below = (rows >> level) > (cols >> level)
        masks_ref[level] = jnp.where(same & below, 1.0, 0.0).astype(BF)
    masks_ref[7] = jnp.where(rows == cols, 1.0, 0.0).astype(BF)
    gain = gain_ref[...]
    pl.semaphore_wait(barrier, len(others))

    st_copies = [
        remote(states_ref.at[me], states_ref.at[me], st_send.at[o], st_recv.at[o], group_peers[o])
        for o in range(GROUP - 1)
    ]
    rw_copies = [
        remote(tile_ref, rewards_ref.at[me], rw_send.at[o], rw_recv.at[o], group_peers[o]) for o in range(GROUP - 1)
    ]
    w1_copies = [
        remote(mine, mine, w1_send.at[t], w1_recv.at[t], at_chip(chip_peers[t])) for t in range(CHIPS - 1)
    ]
    for copy in rw_copies + st_copies + w1_copies:
        copy.start()

    held = all_ref.at[me, core_id]
    far_held = all_ref.at[far, core_id]
    w2_copy = remote(held, held, w2_send, w2_recv, {"sample": far})
    w3_near = [
        remote(held, held, w3_send.at[i], w3_recv.at[i], {"sample": along_z(o)}) for i, o in ((0, 1), (1, 3))
    ]
    w3_far = [
        remote(far_held, far_held, w3_send.at[i], w3_recv.at[i], {"sample": along_z(o)}) for i, o in ((2, 1), (3, 3))
    ]

    def passed(index, half, slot, offset):
        piece = all_ref.at[index, core_id, pl.ds(half * 512, 512)]
        return remote(piece, piece, w3_send.at[slot], w3_recv.at[slot], {"sample": along_z(offset)})

    w3_near_on = [passed(along_z(3), 0, 4, 1), passed(along_z(1), 1, 5, 3)]
    w3_far_on = [passed(far_along_z(3), 0, 6, 1), passed(far_along_z(1), 1, 7, 3)]

    def shared(index, slot):
        piece = all_ref.at[index, core_id]
        return remote(piece, piece, w4_send.at[slot], w4_recv.at[slot], sibling)

    w4_copies = [shared(me, 0), shared(far, 1)]
    w4_copies += [shared(along_z(1), 2), shared(along_z(3), 3), shared(far_along_z(1), 4), shared(far_along_z(3), 5)]
    w4_copies += [shared(along_z(2), 6), shared(far_along_z(2), 7)]

    def shift_at(t):
        m = lax.rem(t, 3)
        return (2 - m + 3 * lax.div(m, 2)) * (1 - lax.div(t, 6))

    def pair_at(t):
        turn = 1 - lax.rem(lax.div(t, 3), 2) - lax.div(t, 7)
        return lax.rem(x + shift_at(t), 4) * 2 + lax.rem(yl + turn, 2)

    wt_copy = remote(weighted_ref, weighted_other_ref, wt_send, wt_recv, sibling)

    def mixed_copy(t):
        return remote(mixed_ref.at[t, 1 - core_id], other_ref.at[t], mx_send.at[t], mx_recv.at[t], sibling)

    def to_row(t):
        target = lax.rem(x + shift_at(t), 4) * 2 + yl
        return remote(gsend_ref.at[t], grecv_ref.at[t], g_send.at[t], g_recv.at[t], at_chip(target))

    def to_column(t):
        return remote(gsend_ref.at[t], grecv_ref.at[t], g_send.at[t], g_recv.at[t], column)

    def forward_step(t):
        pair = pair_at(t)
        raw = small_ref[pair]
        raw_row = iota(raw.shape, 0)
        rate = jnp.where(lax.rem(raw_row, 2) == 0, rate_ref[2 * pair], rate_ref[2 * pair + 1])
        small = raw * -rate
        first = small.astype(BF)
        rest = small - first.astype(F32)
        second = rest.astype(BF)
        third = (rest - second.astype(F32)).astype(BF)
        upper = upper_ref[...]
        running = dot(first, upper) + dot(second, upper) + dot(third, upper)
        by_row = jnp.where(raw_row < 2 * samples, jax.nn.sigmoid(raw), running)
        columns = by_row.T
        causal = rows >= cols
        strict = rows > cols
        diagonal = rows == cols
        systems, belows, scores, rights, queries = [], [], [], [], []
        for s in range(samples):
            q = q_ref[s, :, lane_block(pair, 128)]
            k = k_ref[s, :, lane_block(pair, 128)]
            top = dot(jnp.concatenate([k[:HALF], q[:HALF]], axis=0), k[:HALF], ((1,), (1,)))
            low = dot(jnp.concatenate([k[HALF:], q[HALF:]], axis=0), k, ((1,), (1,)))
            kf = k.astype(F32)
            qf = q.astype(F32)
            row_first = lax.rsqrt(jnp.sum(jnp.where(diagonal, top[:HALF], 0.0), axis=0, keepdims=True) + 1e-6)
            row_second = lax.rsqrt(jnp.sum(jnp.where(diagonal, low[:HALF, HALF:], 0.0), axis=0, keepdims=True) + 1e-6)
            k_col = lax.rsqrt(jnp.sum(kf * kf, axis=1, keepdims=True) + 1e-6)
            q_col = lax.rsqrt(jnp.sum(qf * qf, axis=1, keepdims=True) + 1e-6) * (128 ** -0.5)
            top = top * row_first
            low_first = low[:, :HALF] * row_first
            low_second = low[:, HALF:] * row_second
            v = v_ref[s, :, lane_block(pair, 256)].astype(F32)
            for r in range(2):
                i = 2 * s + r
                beta = columns[:, i:i + 1]
                c_col = columns[:, 2 * samples + i:2 * samples + i + 1]
                c_row = by_row[2 * samples + i:2 * samples + i + 1]
                beta_k = beta * k_col
                f_top = jnp.exp(jnp.where(causal, c_col[:HALF] - c_row[:, :HALF], 0.0))
                f_low = jnp.exp(c_col[HALF:] - c_row[:, :HALF])
                f_end = jnp.exp(jnp.where(causal, c_col[HALF:] - c_row[:, HALF:], 0.0))
                systems.append(jnp.where(strict, f_top * top[:HALF] * beta_k[:HALF], 0.0).astype(BF))
                systems.append(jnp.where(strict, f_end * low_second[:HALF] * beta_k[HALF:], 0.0).astype(BF))
                belows.append((f_low * low_first[:HALF] * beta_k[HALF:]).astype(BF))
                p_top = jnp.where(causal, f_top * top[HALF:] * q_col[:HALF], 0.0)
                p_low = f_low * low_first[HALF:] * q_col[HALF:]
                p_end = jnp.where(causal, f_end * low_second[HALF:] * q_col[HALF:], 0.0)
                scores.append((split(p_top), split(jnp.concatenate([p_low, p_end], axis=1))))
                growth = jnp.exp(c_col)
                rights.append(
                    jnp.concatenate([beta * v[:, 128 * r:128 * r + 128], (growth * beta_k) * kf], axis=1)
                )
                queries.append((growth * q_col) * qf)
        solved = inverses(systems, masks_ref)

        @pl.when(t == 0)
        def _():
            for copy in st_copies:
                copy.wait()

        for s in range(samples):
            gates = g_ref[s, :, lane_block(pair, 256)].astype(F32)
            for r in range(2):
                i = 2 * s + r
                right = rights[i][:HALF]
                first_high, first_low = split(right + dot(solved[2 * i], right.astype(BF)))
                right = rights[i][HALF:] - dot(belows[i], first_high)
                second_high, second_low = split(right + dot(solved[2 * i + 1], right.astype(BF)))
                u_high = jnp.concatenate([first_high, second_high], axis=0)
                u_low = jnp.concatenate([first_low, second_low], axis=0)
                (top_high, top_low), (low_high, low_low) = scores[i]
                pu = jnp.concatenate([
                    dot(top_high, first_high) + (dot(top_low, first_high) + dot(top_high, first_low)),
                    dot(low_high, u_high) + (dot(low_low, u_high) + dot(low_high, u_low)),
                ], axis=0)
                read = (queries[i] - pu[:, 128:]).astype(BF)
                core = pu[:, :128] + dot(read, states_ref[pair, r])
                gate = gates[:, 128 * r:128 * r + 128]
                scale = lax.rsqrt(jnp.mean(core * core, axis=1, keepdims=True) + 1e-6)
                mixed_ref[t, r, pl.ds(s * LEN, LEN)] = (core * scale * gain * (gate * jax.nn.sigmoid(gate))).astype(BF)
                core_ref[pair, r, s] = core.astype(BF)
                read_ref[pair, r, s] = read
        mixed_copy(t).start()

    def weigh():
        for copy in rw_copies:
            copy.wait()
        rewards = rewards_ref[...]
        count = GROUP * samples
        real = iota((GROUP, 8, 128), 1) < samples
        centre = jnp.sum(rewards, axis=(0, 1), keepdims=True) / count
        off = jnp.where(real, rewards - centre, 0.0)
        spread = jnp.sqrt(jnp.sum(off * off, axis=(0, 1), keepdims=True) / count)
        coefficient = ((tile_ref[...] - centre[0]) / jnp.maximum(spread[0], 0.6)) / LEN
        for s in range(samples):
            factor = coefficient[s:s + 1]
            for block in range(16):
                at = pl.ds(block * 128, 128)
                weighted_ref[pl.ds(s * LEN, LEN), at] = (cot_ref[s, :, at].astype(F32) * factor).astype(BF)
        wt_copy.start()

    def partial(t):
        ours = mixed_ref[t, core_id]
        theirs = other_ref[t]
        for block in range(4):
            at = pl.ds(block * 512, 512)
            acc_ref[:, at] = dot(ours, weighted_ref[:, at], ((0,), (0,))) + dot(
                theirs, weighted_other_ref[:, at], ((0,), (0,))
            )

    def gradient_step(t):
        mixed_copy(t).wait()

        @pl.when(t == 0)
        def _():
            wt_copy.wait()

        partial(t)

        @pl.when(t < 6)
        def _():
            gsend_ref[t] = acc_ref[...].astype(BF)
            to_row(t).start()

        @pl.when(t == 6)
        def _():
            total = acc_ref[...]
            for slot in (0, 1, 2):
                to_row(slot).wait()
                total = total + grecv_ref[slot].astype(F32)
            gsend_ref[6] = total.astype(BF)
            to_column(6).start()

    for copy in loads:
        copy.wait()
    weigh()

    def weights_on(t, begin):
        if begin:
            @pl.when(t == 1)
            def _():
                for copy in w1_copies:
                    copy.wait()
                w2_copy.start()
                for copy in w3_near:
                    copy.start()
                w4_copies[0].start()

            @pl.when(t == 3)
            def _():
                w2_copy.wait()
                for copy in w3_far:
                    copy.start()
                w4_copies[1].start()

            @pl.when(t == 4)
            def _():
                for copy in w3_near:
                    copy.wait()
                for copy in w3_near_on:
                    copy.start()
                w4_copies[2].start()
                w4_copies[3].start()

            @pl.when(t == 6)
            def _():
                for copy in w3_near_on:
                    copy.wait()
                w4_copies[6].start()
        else:
            @pl.when(t == 5)
            def _():
                for copy in w3_far:
                    copy.wait()
                for copy in w3_far_on:
                    copy.start()
                w4_copies[4].start()
                w4_copies[5].start()

    def step(t, carry):
        forward_step(t)

        weights_on(t, True)

        @pl.when(t > 0)
        def _():
            gradient_step(t - 1)

        weights_on(t, False)
        return carry

    lax.fori_loop(0, CHIPS, step, 0)
    mixed_copy(7).wait()
    partial(7)
    for copy in w3_far_on:
        copy.wait()
    w4_copies[7].start()

    height = 128 // GROUP

    def slab(index):
        return pl.ds(pl.multiple_of(index * height, height), height)

    s_copies = [
        remote(
            part_ref.at[slab(lax.rem(me + o, GROUP))], slices_ref.at[o - 1], s_send.at[o - 1], s_recv.at[o - 1], in_group(o)
        )
        for o in range(1, GROUP)
    ]
    a_copies = [
        remote(sum_ref, grad_ref.at[slab(me)], a_send.at[o - 1], a_recv.at[o - 1], in_group(o))
        for o in range(1, GROUP)
    ]
    for copy in w4_copies:
        copy.wait()

    def prefix_copy(u):
        return remote(psend_ref.at[u], precv_ref.at[u], p_send.at[u], p_recv.at[u], in_group(u + 1))

    def pair_grads(u):
        pair = lax.rem(me + 1 + u, GROUP)
        back = jnp.zeros((weighted_ref.shape[0], 256), F32)
        for block in range(GROUP):
            piece = all_ref[block, :, lane_block(pair, 128)].reshape(256, 256)
            back = back + dot(weighted_ref[:, block * 256:block * 256 + 256], piece, ((1,), (1,)))
        grads = [jnp.zeros((128, 128), F32), jnp.zeros((128, 128), F32)]
        for s in range(samples):
            gates = g_ref[s, :, lane_block(pair, 256)].astype(F32)
            for r in range(2):
                core = core_ref[pair, r, s].astype(F32)
                gate = gates[:, 128 * r:128 * r + 128]
                scale = lax.rsqrt(jnp.mean(core * core, axis=1, keepdims=True) + 1e-6)
                normed = core * scale
                lifted = back[s * LEN:s * LEN + LEN, 128 * r:128 * r + 128] * gain * (gate * jax.nn.sigmoid(gate))
                core_grad = scale * (lifted - normed * jnp.mean(lifted * normed, axis=1, keepdims=True))
                high, low = split(core_grad)
                read = read_ref[pair, r, s]
                grads[r] = grads[r] + dot(read, high, ((0,), (0,))) + dot(read, low, ((0,), (0,)))
        return grads

    def back_step(u, carry):
        grads = pair_grads(u)
        psend_ref[u, 0] = grads[0].astype(BF)
        psend_ref[u, 1] = grads[1].astype(BF)
        prefix_copy(u).start()

        @pl.when(u == 2)
        def _():
            total = acc_ref[...]
            for slot in (3, 4, 5):
                to_row(slot).wait()
                total = total + grecv_ref[slot].astype(F32)
            to_column(6).wait()
            total = total + grecv_ref[6].astype(F32)
            acc_ref[...] = total
            part_ref[...] = total.astype(BF)
            for copy in s_copies:
                copy.start()

        @pl.when(u == 5)
        def _():
            total = acc_ref[slab(me)]
            for o in range(GROUP - 1):
                s_copies[o].wait()
                total = total + slices_ref[o].astype(F32)
            sum_ref[...] = total
            grad_ref[slab(me)] = total
            for copy in a_copies:
                copy.start()

        return carry

    lax.fori_loop(0, GROUP - 1, back_step, 0)
    own = pair_grads(GROUP - 1)
    for u in range(GROUP - 1):
        prefix_copy(u).wait()
    for r in range(2):
        total = own[r]
        for u in range(GROUP - 1):
            total = total + precv_ref[u, r].astype(F32)
        prefix_ref[r] = total
    for copy in a_copies:
        copy.wait()


def whole(rates, rewards, gain, beta, decay, state, weight, q, k, v, g, cot):
    samples, _, wide = v.shape
    pairs = wide // 256
    tokens = samples * LEN
    dma = pltpu.SemaphoreType.DMA
    vmem = pl.BlockSpec(memory_space=pltpu.VMEM)
    smem = pl.BlockSpec(memory_space=pltpu.SMEM)
    anywhere = pl.BlockSpec(memory_space=pl.ANY)
    sems = [dma((5,))]
    for count in (7, 7, None, 8, 7, 7, None, 8, 8, 7, 7, 7):
        sems += [dma if count is None else dma((count,))] * 2
    return pl.pallas_call(
        functools.partial(whole_kernel, samples),
        in_specs=[smem, smem] + [vmem] * 5 + [anywhere] * 5,
        out_specs=[vmem] * 2,
        out_shape=[
            jax.ShapeDtypeStruct((2, 128, 128), F32),
            jax.ShapeDtypeStruct((128, wide), F32),
        ],
        scratch_shapes=[
            pltpu.VMEM(q.shape, BF),
            pltpu.VMEM(k.shape, BF),
            pltpu.VMEM(v.shape, BF),
            pltpu.VMEM(g.shape, BF),
            pltpu.VMEM(cot.shape, BF),
            pltpu.VMEM((8, HALF, HALF), BF),
            pltpu.VMEM((LEN, LEN), BF),
            pltpu.VMEM((pairs, 4 * samples, LEN), F32),
            pltpu.VMEM((GROUP, 2, 128, 128), BF),
            pltpu.VMEM((GROUP, 8, 128), F32),
            pltpu.VMEM((8, 128), F32),
            pltpu.VMEM((pairs, 2, tokens, 128), BF),
            pltpu.VMEM((pairs, tokens, 128), BF),
            pltpu.VMEM((tokens, wide), BF),
            pltpu.VMEM((tokens, wide), BF),
            pltpu.VMEM((pairs, 2, samples, LEN, 128), BF),
            pltpu.VMEM((pairs, 2, samples, LEN, 128), BF),
            pltpu.VMEM((GROUP, 2, wide // 2, wide // GROUP), BF),
            pltpu.VMEM((7, 128, wide), BF),
            pltpu.VMEM((7, 128, wide), BF),
            pltpu.VMEM((128, wide), F32),
            pltpu.VMEM((128, wide), BF),
            pltpu.VMEM((7, 128 // GROUP, wide), BF),
            pltpu.VMEM((128 // GROUP, wide), F32),
            pltpu.VMEM((7, 2, 128, 128), BF),
            pltpu.VMEM((7, 2, 128, 128), BF),
        ] + sems,
        compiler_params=pltpu.CompilerParams(
            collective_id=0, has_side_effects=True, vmem_limit_bytes=62 * 1024 * 1024
        ),
    )(rates, rewards, gain, beta, decay, state, weight, q, k, v, g, cot)


def adam_update(weight, first_moment, second_moment, gradient):
    first_new = 0.9 * first_moment + 0.1 * gradient
    second_new = 0.95 * second_moment + 0.05 * gradient * gradient
    direction = first_new / (1.0 - 0.9**10) / (jnp.sqrt(second_new / (1.0 - 0.95**10)) + 1e-08)
    weight_new = weight - 0.001 * (direction + 0.1 * weight)
    return (weight_new, first_new, second_new)


def local(
    query_vectors,
    key_vectors,
    value_vectors,
    output_gates,
    beta_logits,
    decay_logits,
    decay_rates,
    norm_gain,
    prefix_states,
    cotangent,
    rewards,
    out_weight,
    first_moment,
    second_moment,
):
    prefix_grad, gradient = whole(
        decay_rates, rewards, norm_gain[None], beta_logits[0], decay_logits[0], prefix_states[0], out_weight,
        query_vectors[0], key_vectors[0], value_vectors[0], output_gates[0], cotangent[0],
    )
    return (prefix_grad[None],) + adam_update(out_weight, first_moment, second_moment, gradient)


def solution(mesh):
    placed = (
        P("dp", "sample", None, None),
        P("dp", "sample", None, None),
        P("dp", "sample", None, None),
        P("dp", "sample", None, None),
        P("dp", "sample", None, None),
        P("dp", "sample", None, None),
        P(),
        P(),
        P("dp", "sample", None, None),
        P("dp", "sample", None, None),
        P("dp", "sample"),
        P("dp", None),
        P("dp", None),
        P("dp", None),
    )
    return jax.shard_map(
        local,
        mesh=mesh,
        in_specs=placed,
        out_specs=(P("dp", "sample", None, None), P("dp", None), P("dp", None), P("dp", None)),
        check_vma=False,
    )
```

```python
import functools
import jax
import jax.numpy as jnp
from jax import lax
from jax.experimental import pallas as pl
from jax.experimental.pallas import tpu as pltpu
from jax.sharding import PartitionSpec as P

LEN = 256
HALF = 128
F32 = jnp.float32
BF = jnp.bfloat16
MESH = pl.DeviceIdType.MESH
CHIPS = 8
GROUP = 8


def dot(a, b, dims=((1,), (0,))):
    return lax.dot_general(a, b, (dims, ((), ())), preferred_element_type=F32)


def iota(shape, dim):
    return lax.broadcasted_iota(jnp.int32, shape, dim)


def split(x):
    high = x.astype(BF)
    return high, (x - high.astype(F32)).astype(BF)


def odd_rows(x, width):
    n = x.shape[0] // (2 * width)
    return x.reshape((n, 2, width) + x.shape[1:])[:, 1].reshape((n * width,) + x.shape[1:])


def put_odd(x, rows, width):
    n = x.shape[0] // (2 * width)
    parted = x.reshape((n, 2, width) + x.shape[1:])
    rows = rows.reshape((n, width) + x.shape[1:])
    return jnp.stack([parted[:, 0], parted[:, 1] - rows], axis=1).reshape(x.shape)


def inverses(systems, masks_ref):
    count = len(systems)
    eye = masks_ref[7]
    results = [eye - a * masks_ref[0] for a in systems]
    for level in range(1, 7):
        width = 1 << level
        mask = masks_ref[level]
        if width < 16:
            lefts = [dot(results[i], systems[i] * mask).astype(BF) for i in range(count)]
            fixes = [dot(lefts[i], results[i]).astype(BF) for i in range(count)]
            results = [results[i] - fixes[i] for i in range(count)]
        else:
            lefts = [dot(odd_rows(results[i], width), systems[i] * mask).astype(BF) for i in range(count)]
            fixes = [dot(lefts[i], results[i]).astype(BF) for i in range(count)]
            results = [put_odd(results[i], fixes[i], width) for i in range(count)]
    return [r - eye for r in results]


def places():
    dp = lax.axis_index("dp")
    return lax.div(dp, 4), lax.rem(lax.div(dp, 2), 2), lax.rem(dp, 2), lax.axis_index("sample")


def remote(src, dst, send, recv, where):
    return pltpu.make_async_remote_copy(
        src_ref=src, dst_ref=dst, send_sem=send, recv_sem=recv, device_id=where, device_id_type=MESH
    )


def lane_block(index, width):
    return pl.ds(pl.multiple_of(index * width, width), width)


def whole_kernel(
    samples, rate_ref, reward_ref, gain_ref, beta_ref, decay_ref, state_ref, weight_ref,
    q_in, k_in, v_in, g_in, cot_in,
    prefix_ref, grad_ref,
    q_ref, k_ref, v_ref, g_ref, cot_ref,
    masks_ref, upper_ref, small_ref, states_ref, rewards_ref, tile_ref, mixed_ref, other_ref, weighted_ref, weighted_other_ref,
    core_ref, read_ref, all_ref, gsend_ref, grecv_ref, acc_ref, part_ref, slices_ref, sum_ref, psend_ref, precv_ref,
    in_sem, st_send, st_recv, rw_send, rw_recv, wt_send, wt_recv, mx_send, mx_recv, g_send, g_recv,
    w1_send, w1_recv, w2_send, w2_recv, w3_send, w3_recv, w4_send, w4_recv,
    s_send, s_recv, a_send, a_recv, p_send, p_recv,
):
    loads = [
        pltpu.make_async_copy(source, target, in_sem.at[i])
        for i, (source, target) in enumerate(
            ((k_in, k_ref), (q_in, q_ref), (v_in, v_ref), (g_in, g_ref), (cot_in, cot_ref))
        )
    ]
    for copy in loads:
        copy.start()
    x, yl, core_id, me = places()
    chip = x * 2 + yl
    y_hi, z = lax.div(me, 4), lax.rem(me, 4)
    far = (1 - y_hi) * 4 + z
    sibling = {"dp": chip * 2 + 1 - core_id, "sample": me}
    column = {"dp": (x * 2 + 1 - yl) * 2 + core_id, "sample": me}

    def at_chip(index):
        return {"dp": index * 2 + core_id, "sample": me}

    def in_group(offset):
        return {"sample": lax.rem(me + offset, GROUP)}

    def along_z(offset):
        return y_hi * 4 + lax.rem(z + offset, 4)

    def far_along_z(offset):
        return (1 - y_hi) * 4 + lax.rem(z + offset, 4)

    chip_peers = [lax.rem(x + t // 2, 4) * 2 + lax.rem(yl + t % 2, 2) for t in range(1, CHIPS)]
    group_peers = [in_group(o) for o in range(1, GROUP)]
    others = [sibling] + [at_chip(c) for c in chip_peers] + group_peers
    barrier = pltpu.get_barrier_semaphore()
    for partner in others:
        pl.semaphore_signal(barrier, inc=1, device_id=partner, device_id_type=MESH)

    states_ref[me] = state_ref[...].astype(BF)
    mine = all_ref.at[me, core_id, lane_block(chip, 128)]
    mine[...] = weight_ref[:, lane_block(me, 256)].astype(BF)
    tile_row = iota((8, 128), 0)
    tile = jnp.zeros((8, 128), F32)
    for s in range(samples):
        tile = jnp.where(tile_row == s, reward_ref[0, s], tile)
    tile_ref[...] = tile
    rewards_ref[me] = tile
    for s in range(samples):
        betas = beta_ref[s].astype(F32)
        softs = jax.nn.softplus(decay_ref[s].astype(F32))
        for pair in range(betas.shape[0] // 2):
            small_ref[pair, 2 * s:2 * s + 2] = betas[2 * pair:2 * pair + 2]
            small_ref[pair, 2 * (samples + s):2 * (samples + s) + 2] = softs[2 * pair:2 * pair + 2]
    upper_ref[...] = jnp.where(iota((LEN, LEN), 0) <= iota((LEN, LEN), 1), 1.0, 0.0).astype(BF)
    rows = iota((HALF, HALF), 0)
    cols = iota((HALF, HALF), 1)
    for level in range(7):
        same = (rows >> (level + 1)) == (cols >> (level + 1))
        below = (rows >> level) > (cols >> level)
        masks_ref[level] = jnp.where(same & below, 1.0, 0.0).astype(BF)
    masks_ref[7] = jnp.where(rows == cols, 1.0, 0.0).astype(BF)
    gain = gain_ref[...]
    pl.semaphore_wait(barrier, len(others))

    st_copies = [
        remote(states_ref.at[me], states_ref.at[me], st_send.at[o], st_recv.at[o], group_peers[o])
        for o in range(GROUP - 1)
    ]
    rw_copies = [
        remote(tile_ref, rewards_ref.at[me], rw_send.at[o], rw_recv.at[o], group_peers[o]) for o in range(GROUP - 1)
    ]
    w1_copies = [
        remote(mine, mine, w1_send.at[t], w1_recv.at[t], at_chip(chip_peers[t])) for t in range(CHIPS - 1)
    ]
    for copy in rw_copies + st_copies + w1_copies:
        copy.start()

    held = all_ref.at[me, core_id]
    far_held = all_ref.at[far, core_id]
    w2_copy = remote(held, held, w2_send, w2_recv, {"sample": far})
    w3_near = [
        remote(held, held, w3_send.at[i], w3_recv.at[i], {"sample": along_z(o)}) for i, o in ((0, 1), (1, 3))
    ]
    w3_far = [
        remote(far_held, far_held, w3_send.at[i], w3_recv.at[i], {"sample": along_z(o)}) for i, o in ((2, 1), (3, 3))
    ]

    def passed(index, half, slot, offset):
        piece = all_ref.at[index, core_id, pl.ds(half * 512, 512)]
        return remote(piece, piece, w3_send.at[slot], w3_recv.at[slot], {"sample": along_z(offset)})

    w3_near_on = [passed(along_z(3), 0, 4, 1), passed(along_z(1), 1, 5, 3)]
    w3_far_on = [passed(far_along_z(3), 0, 6, 1), passed(far_along_z(1), 1, 7, 3)]

    def shared(index, slot):
        piece = all_ref.at[index, core_id]
        return remote(piece, piece, w4_send.at[slot], w4_recv.at[slot], sibling)

    w4_copies = [shared(me, 0), shared(far, 1)]
    w4_copies += [shared(along_z(1), 2), shared(along_z(3), 3), shared(far_along_z(1), 4), shared(far_along_z(3), 5)]
    w4_copies += [shared(along_z(2), 6), shared(far_along_z(2), 7)]

    def shift_at(t):
        m = lax.rem(t, 3)
        return (2 - m + 3 * lax.div(m, 2)) * (1 - lax.div(t, 6))

    def pair_at(t):
        turn = 1 - lax.rem(lax.div(t, 3), 2) - lax.div(t, 7)
        return lax.rem(x + shift_at(t), 4) * 2 + lax.rem(yl + turn, 2)

    wt_copy = remote(weighted_ref, weighted_other_ref, wt_send, wt_recv, sibling)

    def mixed_copy(t):
        return remote(mixed_ref.at[t, 1 - core_id], other_ref.at[t], mx_send.at[t], mx_recv.at[t], sibling)

    def to_row(t):
        target = lax.rem(x + shift_at(t), 4) * 2 + yl
        return remote(gsend_ref.at[t], grecv_ref.at[t], g_send.at[t], g_recv.at[t], at_chip(target))

    def to_column(t):
        return remote(gsend_ref.at[t], grecv_ref.at[t], g_send.at[t], g_recv.at[t], column)

    def forward_step(t):
        pair = pair_at(t)
        raw = small_ref[pair]
        raw_row = iota(raw.shape, 0)
        rate = jnp.where(lax.rem(raw_row, 2) == 0, rate_ref[2 * pair], rate_ref[2 * pair + 1])
        small = raw * -rate
        first = small.astype(BF)
        rest = small - first.astype(F32)
        second = rest.astype(BF)
        third = (rest - second.astype(F32)).astype(BF)
        upper = upper_ref[...]
        running = dot(first, upper) + dot(second, upper) + dot(third, upper)
        by_row = jnp.where(raw_row < 2 * samples, jax.nn.sigmoid(raw), running)
        columns = by_row.T
        causal = rows >= cols
        strict = rows > cols
        diagonal = rows == cols
        systems, belows, scores, rights, queries = [], [], [], [], []
        for s in range(samples):
            q = q_ref[s, :, lane_block(pair, 128)]
            k = k_ref[s, :, lane_block(pair, 128)]
            top = dot(jnp.concatenate([k[:HALF], q[:HALF]], axis=0), k[:HALF], ((1,), (1,)))
            low = dot(jnp.concatenate([k[HALF:], q[HALF:]], axis=0), k, ((1,), (1,)))
            kf = k.astype(F32)
            qf = q.astype(F32)
            row_first = lax.rsqrt(jnp.sum(jnp.where(diagonal, top[:HALF], 0.0), axis=0, keepdims=True) + 1e-6)
            row_second = lax.rsqrt(jnp.sum(jnp.where(diagonal, low[:HALF, HALF:], 0.0), axis=0, keepdims=True) + 1e-6)
            k_col = lax.rsqrt(jnp.sum(kf * kf, axis=1, keepdims=True) + 1e-6)
            q_col = lax.rsqrt(jnp.sum(qf * qf, axis=1, keepdims=True) + 1e-6) * (128 ** -0.5)
            top = top * row_first
            low_first = low[:, :HALF] * row_first
            low_second = low[:, HALF:] * row_second
            v = v_ref[s, :, lane_block(pair, 256)].astype(F32)
            for r in range(2):
                i = 2 * s + r
                beta = columns[:, i:i + 1]
                c_col = columns[:, 2 * samples + i:2 * samples + i + 1]
                c_row = by_row[2 * samples + i:2 * samples + i + 1]
                beta_k = beta * k_col
                f_top = jnp.exp(jnp.where(causal, c_col[:HALF] - c_row[:, :HALF], 0.0))
                f_low = jnp.exp(c_col[HALF:] - c_row[:, :HALF])
                f_end = jnp.exp(jnp.where(causal, c_col[HALF:] - c_row[:, HALF:], 0.0))
                systems.append(jnp.where(strict, f_top * top[:HALF] * beta_k[:HALF], 0.0).astype(BF))
                systems.append(jnp.where(strict, f_end * low_second[:HALF] * beta_k[HALF:], 0.0).astype(BF))
                belows.append((f_low * low_first[:HALF] * beta_k[HALF:]).astype(BF))
                p_top = jnp.where(causal, f_top * top[HALF:] * q_col[:HALF], 0.0)
                p_low = f_low * low_first[HALF:] * q_col[HALF:]
                p_end = jnp.where(causal, f_end * low_second[HALF:] * q_col[HALF:], 0.0)
                scores.append((split(p_top), split(jnp.concatenate([p_low, p_end], axis=1))))
                growth = jnp.exp(c_col)
                rights.append(
                    jnp.concatenate([beta * v[:, 128 * r:128 * r + 128], (growth * beta_k) * kf], axis=1)
                )
                queries.append((growth * q_col) * qf)
        solved = inverses(systems, masks_ref)

        if isinstance(t, int):
            for copy in st_copies:
                copy.wait()
            for copy in w1_copies:
                copy.wait()
            w2_copy.start()
            for copy in w3_near:
                copy.start()
            w4_copies[0].start()

        for s in range(samples):
            gates = g_ref[s, :, lane_block(pair, 256)].astype(F32)
            for r in range(2):
                i = 2 * s + r
                right = rights[i][:HALF]
                first_high, first_low = split(right + dot(solved[2 * i], right.astype(BF)))
                right = rights[i][HALF:] - dot(belows[i], first_high)
                second_high, second_low = split(right + dot(solved[2 * i + 1], right.astype(BF)))
                u_high = jnp.concatenate([first_high, second_high], axis=0)
                u_low = jnp.concatenate([first_low, second_low], axis=0)
                (top_high, top_low), (low_high, low_low) = scores[i]
                pu = jnp.concatenate([
                    dot(top_high, first_high) + (dot(top_low, first_high) + dot(top_high, first_low)),
                    dot(low_high, u_high) + (dot(low_low, u_high) + dot(low_high, u_low)),
                ], axis=0)
                read = (queries[i] - pu[:, 128:]).astype(BF)
                core = pu[:, :128] + dot(read, states_ref[pair, r])
                gate = gates[:, 128 * r:128 * r + 128]
                scale = lax.rsqrt(jnp.mean(core * core, axis=1, keepdims=True) + 1e-6)
                mixed_ref[t, r, pl.ds(s * LEN, LEN)] = (core * scale * gain * (gate * jax.nn.sigmoid(gate))).astype(BF)
                core_ref[pair, r, s] = core.astype(BF)
                read_ref[pair, r, s] = read
        mixed_copy(t).start()

    def weigh():
        for copy in rw_copies:
            copy.wait()
        rewards = rewards_ref[...]
        count = GROUP * samples
        real = iota((GROUP, 8, 128), 1) < samples
        centre = jnp.sum(rewards, axis=(0, 1), keepdims=True) / count
        off = jnp.where(real, rewards - centre, 0.0)
        spread = jnp.sqrt(jnp.sum(off * off, axis=(0, 1), keepdims=True) / count)
        coefficient = ((tile_ref[...] - centre[0]) / jnp.maximum(spread[0], 0.6)) / LEN
        for s in range(samples):
            factor = coefficient[s:s + 1]
            for block in range(16):
                at = pl.ds(block * 128, 128)
                weighted_ref[pl.ds(s * LEN, LEN), at] = (cot_ref[s, :, at].astype(F32) * factor).astype(BF)
        wt_copy.start()

    def partial(t):
        both = jnp.concatenate([mixed_ref[t, core_id], other_ref[t]], axis=0).T
        for block in range(4):
            at = pl.ds(block * 512, 512)
            acc_ref[:, at] = dot(both, jnp.concatenate([weighted_ref[:, at], weighted_other_ref[:, at]], axis=0))

    def gradient_step(t):
        mixed_copy(t).wait()

        @pl.when(t == 0)
        def _():
            wt_copy.wait()

        partial(t)

        @pl.when(t == 0)
        def _():
            gsend_ref[0] = acc_ref[...].astype(BF)
            to_column(0).start()

        @pl.when(t == 3)
        def _():
            to_column(0).wait()
            gsend_ref[3] = (acc_ref[...] + grecv_ref[0].astype(F32)).astype(BF)
            to_row(3).start()

        @pl.when((t > 0) & (t < 6) & (t != 3))
        def _():
            gsend_ref[t] = acc_ref[...].astype(BF)
            to_row(t).start()

        @pl.when(t == 6)
        def _():
            total = acc_ref[...]
            for slot in (1, 2):
                to_row(slot).wait()
                total = total + grecv_ref[slot].astype(F32)
            gsend_ref[6] = total.astype(BF)
            to_column(6).start()

    for copy in loads:
        copy.wait()
    weigh()

    def step(t, carry):
        forward_step(t)

        gradient_step(t - 1)

        @pl.when(t == 3)
        def _():
            for copy in w3_near:
                copy.wait()
            for copy in w3_near_on:
                copy.start()
            w4_copies[2].start()
            w4_copies[3].start()

        @pl.when(t == 5)
        def _():
            for copy in w3_near_on:
                copy.wait()
            w4_copies[6].start()

        @pl.when(t == 2)
        def _():
            w2_copy.wait()
            for copy in w3_far:
                copy.start()
            w4_copies[1].start()

        @pl.when(t == 4)
        def _():
            for copy in w3_far:
                copy.wait()
            for copy in w3_far_on:
                copy.start()
            w4_copies[4].start()
            w4_copies[5].start()

        return carry

    forward_step(0)
    lax.fori_loop(1, CHIPS, step, 0)
    mixed_copy(7).wait()
    partial(7)
    for copy in w3_far_on:
        copy.wait()
    w4_copies[7].start()

    height = 128 // GROUP

    def slab(index):
        return pl.ds(pl.multiple_of(index * height, height), height)

    s_copies = [
        remote(
            part_ref.at[slab(lax.rem(me + o, GROUP))], slices_ref.at[o - 1], s_send.at[o - 1], s_recv.at[o - 1], in_group(o)
        )
        for o in range(1, GROUP)
    ]
    a_copies = [
        remote(sum_ref, grad_ref.at[slab(me)], a_send.at[o - 1], a_recv.at[o - 1], in_group(o))
        for o in range(1, GROUP)
    ]
    for copy in w4_copies:
        copy.wait()

    def prefix_copy(u):
        return remote(psend_ref.at[u], precv_ref.at[u], p_send.at[u], p_recv.at[u], in_group(u + 1))

    def pair_grads(u):
        pair = lax.rem(me + 1 + u, GROUP)
        pieces = [all_ref[block, :, lane_block(pair, 128)].reshape(256, 256) for block in range(GROUP)]
        back = dot(weighted_ref[...], jnp.concatenate(pieces, axis=1), ((1,), (1,)))
        grads = [jnp.zeros((128, 128), F32), jnp.zeros((128, 128), F32)]
        for s in range(samples):
            gates = g_ref[s, :, lane_block(pair, 256)].astype(F32)
            for r in range(2):
                core = core_ref[pair, r, s].astype(F32)
                gate = gates[:, 128 * r:128 * r + 128]
                scale = lax.rsqrt(jnp.mean(core * core, axis=1, keepdims=True) + 1e-6)
                normed = core * scale
                lifted = back[s * LEN:s * LEN + LEN, 128 * r:128 * r + 128] * gain * (gate * jax.nn.sigmoid(gate))
                core_grad = scale * (lifted - normed * jnp.mean(lifted * normed, axis=1, keepdims=True))
                high, low = split(core_grad)
                read = read_ref[pair, r, s]
                grads[r] = grads[r] + dot(read, high, ((0,), (0,))) + dot(read, low, ((0,), (0,)))
        return grads

    def back_step(u, carry):
        grads = pair_grads(u)
        psend_ref[u, 0] = grads[0].astype(BF)
        psend_ref[u, 1] = grads[1].astype(BF)
        prefix_copy(u).start()

        @pl.when(u == 3)
        def _():
            total = acc_ref[...]
            for slot in (3, 4, 5):
                to_row(slot).wait()
                total = total + grecv_ref[slot].astype(F32)
            to_column(6).wait()
            total = total + grecv_ref[6].astype(F32)
            acc_ref[...] = total
            part_ref[...] = total.astype(BF)
            for copy in s_copies:
                copy.start()

        @pl.when(u == 6)
        def _():
            total = acc_ref[slab(me)]
            for o in range(GROUP - 1):
                s_copies[o].wait()
                total = total + slices_ref[o].astype(F32)
            sum_ref[...] = total
            grad_ref[slab(me)] = total
            for copy in a_copies:
                copy.start()

        return carry

    lax.fori_loop(0, GROUP - 1, back_step, 0)
    own = pair_grads(GROUP - 1)
    for u in range(GROUP - 1):
        prefix_copy(u).wait()
    for r in range(2):
        total = own[r]
        for u in range(GROUP - 1):
            total = total + precv_ref[u, r].astype(F32)
        prefix_ref[r] = total
    for copy in a_copies:
        copy.wait()


def whole(rates, rewards, gain, beta, decay, state, weight, q, k, v, g, cot):
    samples, _, wide = v.shape
    pairs = wide // 256
    tokens = samples * LEN
    dma = pltpu.SemaphoreType.DMA
    vmem = pl.BlockSpec(memory_space=pltpu.VMEM)
    smem = pl.BlockSpec(memory_space=pltpu.SMEM)
    anywhere = pl.BlockSpec(memory_space=pl.ANY)
    sems = [dma((5,))]
    for count in (7, 7, None, 8, 7, 7, None, 8, 8, 7, 7, 7):
        sems += [dma if count is None else dma((count,))] * 2
    return pl.pallas_call(
        functools.partial(whole_kernel, samples),
        in_specs=[smem, smem] + [vmem] * 5 + [anywhere] * 5,
        out_specs=[vmem] * 2,
        out_shape=[
            jax.ShapeDtypeStruct((2, 128, 128), F32),
            jax.ShapeDtypeStruct((128, wide), F32),
        ],
        scratch_shapes=[
            pltpu.VMEM(q.shape, BF),
            pltpu.VMEM(k.shape, BF),
            pltpu.VMEM(v.shape, BF),
            pltpu.VMEM(g.shape, BF),
            pltpu.VMEM(cot.shape, BF),
            pltpu.VMEM((8, HALF, HALF), BF),
            pltpu.VMEM((LEN, LEN), BF),
            pltpu.VMEM((pairs, 4 * samples, LEN), F32),
            pltpu.VMEM((GROUP, 2, 128, 128), BF),
            pltpu.VMEM((GROUP, 8, 128), F32),
            pltpu.VMEM((8, 128), F32),
            pltpu.VMEM((pairs, 2, tokens, 128), BF),
            pltpu.VMEM((pairs, tokens, 128), BF),
            pltpu.VMEM((tokens, wide), BF),
            pltpu.VMEM((tokens, wide), BF),
            pltpu.VMEM((pairs, 2, samples, LEN, 128), BF),
            pltpu.VMEM((pairs, 2, samples, LEN, 128), BF),
            pltpu.VMEM((GROUP, 2, wide // 2, wide // GROUP), BF),
            pltpu.VMEM((7, 128, wide), BF),
            pltpu.VMEM((7, 128, wide), BF),
            pltpu.VMEM((128, wide), F32),
            pltpu.VMEM((128, wide), BF),
            pltpu.VMEM((7, 128 // GROUP, wide), BF),
            pltpu.VMEM((128 // GROUP, wide), F32),
            pltpu.VMEM((7, 2, 128, 128), BF),
            pltpu.VMEM((7, 2, 128, 128), BF),
        ] + sems,
        compiler_params=pltpu.CompilerParams(
            collective_id=0, has_side_effects=True, vmem_limit_bytes=62 * 1024 * 1024
        ),
    )(rates, rewards, gain, beta, decay, state, weight, q, k, v, g, cot)


def adam_update(weight, first_moment, second_moment, gradient):
    first_new = 0.9 * first_moment + 0.1 * gradient
    second_new = 0.95 * second_moment + 0.05 * gradient * gradient
    direction = first_new / (1.0 - 0.9**10) / (jnp.sqrt(second_new / (1.0 - 0.95**10)) + 1e-08)
    weight_new = weight - 0.001 * (direction + 0.1 * weight)
    return (weight_new, first_new, second_new)


def local(
    query_vectors,
    key_vectors,
    value_vectors,
    output_gates,
    beta_logits,
    decay_logits,
    decay_rates,
    norm_gain,
    prefix_states,
    cotangent,
    rewards,
    out_weight,
    first_moment,
    second_moment,
):
    prefix_grad, gradient = whole(
        decay_rates, rewards, norm_gain[None], beta_logits[0], decay_logits[0], prefix_states[0], out_weight,
        query_vectors[0], key_vectors[0], value_vectors[0], output_gates[0], cotangent[0],
    )
    return (prefix_grad[None],) + adam_update(out_weight, first_moment, second_moment, gradient)


def solution(mesh):
    placed = (
        P("dp", "sample", None, None),
        P("dp", "sample", None, None),
        P("dp", "sample", None, None),
        P("dp", "sample", None, None),
        P("dp", "sample", None, None),
        P("dp", "sample", None, None),
        P(),
        P(),
        P("dp", "sample", None, None),
        P("dp", "sample", None, None),
        P("dp", "sample"),
        P("dp", None),
        P("dp", None),
        P("dp", None),
    )
    return jax.shard_map(
        local,
        mesh=mesh,
        in_specs=placed,
        out_specs=(P("dp", "sample", None, None), P("dp", None), P("dp", None), P("dp", None)),
        check_vma=False,
    )
```
